256 devices in a mesh: cp: 32 (over y, z), tp: 8 (over x, core).
Axes of the slice: x: 4, y: 4, z: 8, core: 2. Of those that a mesh axis runs over, the one named last changes fastest.
Arguments:
- queries: bfloat16 [12288, 4096], P('cp', 'tp'), may hold values from -36 to 36
- keys: bfloat16 [12288, 1024], P('cp', 'tp'), may hold values from -6 to 6
- values: bfloat16 [12288, 1024], P('cp', 'tp'), may hold values from -18 to 18
- doc_lengths: int32 [4], replicated, may hold values from 1 to 4096, 8192 in all
- shard_starts: int32 [32], replicated, may hold values from 0 to 8000, as said below
- norm_gain: float32 [4096], replicated, may hold values from 0.1 to 1.9
- ffn_weight: bfloat16 [4096, 14336], P('cp', 'tp'), may hold values from -0.09375 to 0.09375
Outputs:
- ffn_out: bfloat16 [8192, 14336], P('cp', 'tp')
The draws below stay inside these ranges and needn't reach their ends.
Inputs may be any that keep to these rules, and one draw needn't show every extreme that they name: `doc_lengths`: each of the 4 documents has at least one token; the longest has exactly 4096. shard_starts[0] = 0, the last start is exactly 64 past its index times 256, and shard_starts[c] differs from c * 256 by at most 64, so every shard holds 128 to 384 tokens, at most 64 of them owned by index c - 1 and at most 64 by index c + 1 of cp; in every draw some shard holds exactly 384 tokens and hands exactly 64 to each of those two owners.
All inputs are finite; a program needn't handle non-finite values.
Results may differ from the reference program's by a relative error of at most 0.017.
Values may be sent and summed in bfloat16 or wider, within the bound.
No kernel may reach another device: no remote copies, remote signals or barrier semaphores. Data moves between devices by JAX's collectives and lax.ppermute only.
A program may use at most 128 MiB of HBM per device.

```python
import math
import jax
import jax.numpy as jnp
import numpy as np
from jax import lax

HEADS = 32
KV = 8
HD = 128
FF = 14336
TOK = 256
NDOCS = 4
D = 4096
CAP = 384
TOKENS = 8192
DOC_MAX = 4096
SLOTS = 12288
N_CP = 32


def shared_rows(key):
    base = jax.random.normal(jax.random.fold_in(key, 101), (SLOTS, KV * HD), jnp.float32)
    return jnp.clip(base, -6.0, 6.0)


def draw_queries(key, part):
    key = jax.random.fold_in(key, 3)
    return jnp.clip(jax.random.normal(key, (SLOTS, HEADS * HD), jnp.float32), -6.0, 6.0).astype(jnp.bfloat16)


def draw_keys(key, part):
    base = shared_rows(key)
    return base.astype(jnp.bfloat16)


def draw_values(key, part):
    key = jax.random.fold_in(key, 5)
    ramp = 1.0 + 2.0 * jnp.arange(KV * HD, dtype=jnp.float32) / (KV * HD - 1)
    draws = jnp.clip(jax.random.normal(key, (SLOTS, KV * HD), jnp.float32), -6.0, 6.0)
    return (draws * ramp).astype(jnp.bfloat16)


def draw_shard_starts(key, part):
    key = jax.random.fold_in(key, 7)
    quarter = TOK // 4
    offsets = jax.random.randint(jax.random.fold_in(key, 1), (N_CP,), -quarter, quarter + 1)
    marked = jax.random.randint(jax.random.fold_in(key, 2), (), 1, N_CP - 1)
    places = jnp.arange(N_CP, dtype=jnp.int32)
    offsets = jnp.where(places == marked, -quarter, offsets)
    offsets = jnp.where(places == marked + 1, quarter, offsets)
    offsets = jnp.where(places == N_CP - 1, quarter, offsets)
    offsets = jnp.where(places == 0, 0, offsets)
    return (places * TOK + offsets).astype(jnp.int32)


def block_scale(rng, extent, shards, least, largest):
    def one(dim, parts):
        heights = jax.random.uniform(jax.random.fold_in(jax.random.fold_in(rng, 6), dim), (parts,), jnp.float32, least / len(shards), largest / len(shards))
        return jnp.repeat(jnp.exp(heights), extent[dim] // parts).reshape((-1,) + (1,) * (len(extent) - dim - 1))

    loudness = one(*shards[0])
    for cut in shards[1:]:
        loudness = loudness * one(*cut)
    return loudness


def profile(number_of, total, most, slope):
    portions = [(1 << 20) // math.isqrt(rank ** slope) + 1 for rank in range(2, number_of + 1)]
    spare, given = total - most - (number_of - 1), [1] * (number_of - 1)
    while spare > 0:
        free = [i for i in range(number_of - 1) if given[i] < most]
        whole, left = sum([portions[i] for i in free]), spare
        for i in free:
            extra = min(most - given[i], max(1, left * portions[i] // whole), spare)
            given[i] = given[i] + extra
            spare = spare - extra
    return np.array([most] + given)


def ragged_sizes(key, count, total, reach, lean):
    if count == 2:
        one = jax.random.randint(key, (), max(1, total - reach), min(reach, total - 1) + 1)
        return jnp.stack([one, total - one])
    lengths = jnp.asarray(profile(count, total, reach, lean), jnp.int32)
    twos = (count - 1) // 2
    giver, receiver = lengths[1:1 + 2 * twos:2], lengths[2:2 + 2 * twos:2]
    slack = jnp.minimum(giver - 1, reach - receiver)
    moved = jax.random.randint(jax.random.fold_in(key, 1), (twos,), 0, 1 << 20) % (slack + 1)
    lengths = lengths.at[1:1 + 2 * twos:2].set(giver - moved).at[2:2 + 2 * twos:2].set(receiver + moved)
    return lengths[jax.random.permutation(jax.random.fold_in(key, 2), count)]


def noise(own_key, shape, deviation, bound, split=(), held_as=jnp.bfloat16):
    loudness = block_scale(own_key, shape, split, -0.22, 0.18) if split else 1.0
    array = jax.random.normal(own_key, shape, jnp.float32) * deviation * loudness
    return jnp.minimum(jnp.maximum(array, -bound), bound).astype(held_as)


def setup_inputs(seed: int = 0) -> dict:
    arg_keys = jax.random.split(jax.random.key(seed), 8)
    return {
        "queries": draw_queries(jax.random.fold_in(arg_keys[7], 71), 0),
        "keys": draw_keys(jax.random.fold_in(arg_keys[7], 71), 0),
        "values": draw_values(jax.random.fold_in(arg_keys[7], 71), 0),
        "doc_lengths": ragged_sizes(arg_keys[3], NDOCS, TOKENS, DOC_MAX, 1).astype(jnp.int32),
        "shard_starts": draw_shard_starts(jax.random.fold_in(arg_keys[7], 71), 0),
        "norm_gain": jnp.clip(1.0 + 0.18 * jax.random.normal(arg_keys[5], (D,), jnp.float32), 0.1, 1.9),
        "ffn_weight": noise(arg_keys[6], (D, FF), D ** -0.5, 0.09375, ((0, 32), (1, 8))),
    }


masked_score = -1e+30
norm_eps = 1e-05

def doc_number(token_ids, doc_ends):
    return lax.optimization_barrier(jnp.sum((doc_ends[None, :] <= token_ids[:, None]).astype(jnp.int32), axis=1)).astype(jnp.int32)

def reference(queries, keys, values, doc_lengths, shard_starts, norm_gain, ffn_weight):
    token_ids = jnp.arange(TOKENS, dtype=jnp.int32)
    owner_shard = (lax.optimization_barrier(jnp.sum((shard_starts[None, :] <= token_ids[:, None]).astype(jnp.int32), axis=1)) - 1).astype(jnp.int32)
    source_rows = (owner_shard * CAP + token_ids - shard_starts[owner_shard]).astype(jnp.int32)
    packed_q = jnp.take(queries, source_rows, axis=0)
    packed_k = jnp.take(keys, source_rows, axis=0)
    packed_v = jnp.take(values, source_rows, axis=0)
    doc_ends = jnp.cumsum(doc_lengths).astype(jnp.int32)
    docs = doc_number(token_ids, doc_ends)
    key_pad = jnp.concatenate([jnp.zeros((DOC_MAX, KV * HD), keys.dtype), packed_k])
    value_pad = jnp.concatenate([jnp.zeros((DOC_MAX, KV * HD), values.dtype), packed_v])
    ident_pad = jnp.concatenate([jnp.full((DOC_MAX,), -1, jnp.int32), token_ids])
    docs_pad = jnp.concatenate([jnp.full((DOC_MAX,), -1, jnp.int32), docs])
    group = HEADS // KV
    scale = HD ** (-0.5)

    def block_out(index):
        first = (index * TOK).astype(jnp.int32)
        query_block = lax.dynamic_slice_in_dim(packed_q, first, TOK, 0).astype(jnp.float32).reshape(TOK, KV, group, HD)
        key_block = lax.dynamic_slice_in_dim(key_pad, first, TOK + DOC_MAX, 0).astype(jnp.float32).reshape(TOK + DOC_MAX, KV, HD)
        value_block = lax.dynamic_slice_in_dim(value_pad, first, TOK + DOC_MAX, 0).astype(jnp.float32).reshape(TOK + DOC_MAX, KV, HD)
        query_ids = lax.dynamic_slice_in_dim(token_ids, first, TOK, 0)
        query_docs = lax.dynamic_slice_in_dim(docs, first, TOK, 0)
        key_ids = lax.dynamic_slice_in_dim(ident_pad, first, TOK + DOC_MAX, 0)
        key_docs = lax.dynamic_slice_in_dim(docs_pad, first, TOK + DOC_MAX, 0)
        allowed = (key_ids[None, :] >= 0) & (key_docs[None, :] == query_docs[:, None]) & (key_ids[None, :] <= query_ids[:, None])
        scores = jnp.einsum('qkgd,pkd->kgqp', query_block, key_block) * scale
        scores = jnp.where(allowed[None, None], scores, masked_score)
        highest = lax.optimization_barrier(jnp.max(scores, axis=-1))
        weights = jnp.exp(scores - highest[..., None])
        mass = lax.optimization_barrier(jnp.sum(weights, axis=-1))
        rounded = lax.optimization_barrier(weights.astype(jnp.bfloat16)).astype(jnp.float32)
        summed = jnp.einsum('kgqp,pkd->qkgd', rounded, value_block)
        return (summed / jnp.transpose(mass, (2, 0, 1))[..., None]).reshape(TOK, HEADS * HD).astype(jnp.bfloat16)
    attended = lax.map(block_out, jnp.arange(N_CP, dtype=jnp.int32)).reshape(TOKENS, HEADS * HD)
    wide = attended.astype(jnp.float32)
    inv_rms = lax.rsqrt(lax.optimization_barrier(jnp.mean(wide * wide, axis=1)) + norm_eps)
    normed = (wide * inv_rms[:, None] * norm_gain).astype(jnp.bfloat16)
    gate = jnp.dot(normed, ffn_weight, preferred_element_type=jnp.float32)
    return jax.nn.silu(gate).astype(jnp.bfloat16)
```

```python
import functools

import jax
import jax.numpy as jnp
from jax import lax
from jax.experimental import pallas as pl
from jax.experimental.pallas import tpu as pltpu
from jax.sharding import Mesh, PartitionSpec as P

HD = 128
TOK = 256
CAP = 384
QUARTER = TOK // 4
FEATURES = 4096
NY, NZ, NX, NC = 4, 8, 4, 2
HEADS_HERE = 4
NORM_EPS = 1e-05
MASKED = -1e30
LOG2E = 1.4426950408889634
EXP2_SCALE = HD ** (-0.5) * LOG2E
RING_COLUMNS = 1024
VMEM = pl.BlockSpec(memory_space=pltpu.VMEM)
SMEM = pl.BlockSpec(memory_space=pltpu.SMEM)


def shift(block, axis, distance):
    count = lax.axis_size(axis)
    return lax.ppermute(block, axis, [(i, (i + distance) % count) for i in range(count)])


def shift_cp(block, distance):
    count = NY * NZ
    return lax.ppermute(block, ("y", "z"), [(i, (i + distance) % count) for i in range(count)])


def z_ring(block, halve_last):
    up, down = [block], [block]
    for _ in range(3):
        up.append(shift(up[-1], "z", 1))
        down.append(shift(down[-1], "z", -1))
    if halve_last:
        half = block.shape[0] // 2
        far = [shift(up[-1][:half], "z", 1), shift(down[-1][half:], "z", -1)]
    else:
        far = [shift(up[-1], "z", 1)]
    return jnp.concatenate(far + [up[3], up[2], up[1], block, down[1], down[2], down[3]], axis=0)


def align_kernel(meta, q, k, v, low, high, q_out, k_out, v_out):
    first, end = meta[0], meta[1]
    row = lax.broadcasted_iota(jnp.int32, (TOK, 1), 0)
    slot = lax.broadcasted_iota(jnp.int32, (TOK, CAP), 1)
    near = lax.broadcasted_iota(jnp.int32, (TOK, QUARTER), 1)
    own = ((slot == row - first) & (row >= first) & (row < end)).astype(jnp.bfloat16)
    from_low = ((near == row) & (row < first)).astype(jnp.bfloat16)
    from_high = ((near == row - end) & (row >= end)).astype(jnp.bfloat16)

    def pick(ref, start, width):
        total = jnp.dot(own, ref[...], preferred_element_type=jnp.float32)
        total += jnp.dot(from_low, low[:, start : start + width], preferred_element_type=jnp.float32)
        total += jnp.dot(from_high, high[:, start : start + width], preferred_element_type=jnp.float32)
        return total.astype(jnp.bfloat16)

    q_out[...] = pick(q, 0, HEADS_HERE * HD)
    k_out[...] = pick(k, HEADS_HERE * HD, HD)
    v_out[...] = pick(v, (HEADS_HERE + 1) * HD, HD)


def align(meta, q, k, v, low, high):
    shape = lambda n: jax.ShapeDtypeStruct((TOK, n), jnp.bfloat16)
    return pl.pallas_call(
        align_kernel,
        out_shape=(shape(HEADS_HERE * HD), shape(HD), shape(HD)),
        in_specs=[SMEM] + [VMEM] * 5,
        out_specs=(VMEM,) * 3,
        compiler_params=pltpu.CompilerParams(vmem_limit_bytes=32 << 20),
    )(meta, q, k, v, low, high)


def attention_kernel(meta, q_ref, k0, k1, k2, v_ref, out_ref, high_ref, mass_ref, sum_ref):
    y, z = meta[2], meta[3]
    ends = [meta[4], meta[5], meta[6], meta[7]]
    mine = y * NZ + z
    query = mine * TOK + lax.broadcasted_iota(jnp.int32, (1, TOK), 1)

    def start_of(token):
        start = token * 0
        for end in ends:
            start = jnp.maximum(start, jnp.where(end <= token, end, 0))
        return start

    starts = start_of(query)
    lowest = start_of(mine * TOK) // TOK
    clear = (start_of(mine * TOK + TOK - 1) + TOK - 1) // TOK

    def step(key, value, block, masked, opening):
        if masked:
            ids = block * TOK + lax.broadcasted_iota(jnp.int32, (TOK, 1), 0)
            allowed = (ids >= starts) & (ids <= query)
        for h in range(HEADS_HERE):
            scores = lax.dot_general(
                key, q_ref[:, h * HD : (h + 1) * HD], (((1,), (1,)), ((), ())), preferred_element_type=jnp.float32
            ) * EXP2_SCALE
            if masked:
                scores = jnp.where(allowed, scores, MASKED)
            top = jnp.max(scores, axis=0, keepdims=True)
            if not opening:
                top = jnp.maximum(top, high_ref[h])
            weights = jnp.exp2(scores - top)
            part = jnp.sum(weights, axis=0, keepdims=True)
            summed = lax.dot_general(
                value, weights.astype(jnp.bfloat16), (((0,), (0,)), ((), ())), preferred_element_type=jnp.float32
            )
            if not opening:
                fading = jnp.exp2(high_ref[h] - top)
                part += mass_ref[h] * fading
                summed += sum_ref[h] * fading
            high_ref[h] = top
            mass_ref[h] = part
            sum_ref[h] = summed

    def at(block):
        return lax.rem(block - y * NZ - z + 4 + 4 * NZ, NZ)

    step(k0[4], v_ref[4, 0], mine, True, True)
    for r, k_ref in enumerate((k0, k1, k2)):
        base = (y - r) * NZ
        low = jnp.maximum(lowest, base)
        high = jnp.minimum(mine, base + NZ)
        middle = jnp.clip(clear, low, jnp.maximum(high, low))

        def body(block, _, k_ref=k_ref, r=r, masked=False):
            p = at(block)
            step(k_ref[p], v_ref[p, r], block, masked, False)
            return 0

        lax.fori_loop(low, jnp.minimum(middle, high), functools.partial(body, masked=True), 0)
        lax.fori_loop(middle, high, body, 0)
    for h in range(HEADS_HERE):
        out_ref[:, h * HD : (h + 1) * HD] = (sum_ref[h] / mass_ref[h]).T.astype(jnp.bfloat16)


def attention(meta, q, k0, k1, k2, v):
    return pl.pallas_call(
        attention_kernel,
        out_shape=jax.ShapeDtypeStruct((TOK, HEADS_HERE * HD), jnp.bfloat16),
        in_specs=[SMEM] + [VMEM] * 5,
        out_specs=VMEM,
        scratch_shapes=[
            pltpu.VMEM((HEADS_HERE, 1, TOK), jnp.float32),
            pltpu.VMEM((HEADS_HERE, 1, TOK), jnp.float32),
            pltpu.VMEM((HEADS_HERE, HD, TOK), jnp.float32),
        ],
        compiler_params=pltpu.CompilerParams(vmem_limit_bytes=40 << 20),
        cost_estimate=pl.CostEstimate(
            flops=17 * 4 * HEADS_HERE * TOK * TOK * HD, bytes_accessed=7 << 20, transcendentals=17 * HEADS_HERE * TOK * TOK
        ),
    )(meta, q, k0, k1, k2, v)


def prepare_kernel(meta, gain, *refs):
    pieces, (plain, moved, inv) = refs[:8], refs[8:]
    y, z, x, c = meta[2], meta[3], meta[8], meta[9]
    squares = jnp.zeros((TOK, HD), jnp.float32)
    for i, piece in enumerate(pieces):
        tp = lax.rem(x + (0, 3, 1, 2)[i // 2], NX) * NC + (c if i % 2 == 0 else 1 - c)
        for j in range(HEADS_HERE):
            head = tp * HEADS_HERE + j
            rows = piece[:, j * HD : (j + 1) * HD].astype(jnp.float32)
            squares += rows * rows
            scaled = (rows * gain[:, pl.ds(pl.multiple_of(head * HD, HD), HD)]).astype(jnp.bfloat16)
            plain[:, pl.ds(pl.multiple_of(head * HD, HD), HD)] = scaled
            dy = lax.rem(head // NZ - y + NY, NY)
            part = jnp.where(dy == 0, 0, jnp.where(dy == 3, 1, dy + 1))
            place = part * NZ + lax.rem(lax.rem(head, NZ) - z + 4 + NZ, NZ)
            moved[:, pl.ds(pl.multiple_of(place * HD, HD), HD)] = scaled
    mean = jnp.sum(squares, axis=1, keepdims=True) / FEATURES
    inv[...] = jnp.broadcast_to(lax.rsqrt(mean + NORM_EPS), (TOK, HD))


def prepare(meta, gain, pieces):
    shape = jax.ShapeDtypeStruct((TOK, FEATURES), jnp.bfloat16)
    return pl.pallas_call(
        prepare_kernel,
        out_shape=(shape, shape, jax.ShapeDtypeStruct((TOK, HD), jnp.float32)),
        in_specs=[SMEM] + [VMEM] * 9,
        out_specs=(VMEM,) * 3,
        compiler_params=pltpu.CompilerParams(vmem_limit_bytes=32 << 20),
    )(meta, gain, *pieces)


def gate_kernel(depths, rows, inv, *refs):
    out = refs[-1]
    total, start = None, 0
    for depth, part in zip(depths, refs):
        term = jnp.dot(rows[:, start : start + depth], part[...], preferred_element_type=jnp.float32)
        total = term if total is None else total + term
        start += depth
    gate = total * inv[:, :1]
    out[...] = (gate / (1.0 + jnp.exp(-gate))).astype(jnp.bfloat16)


def gate(rows, inv, parts, before, first, width, step):
    depths = [part.shape[0] for part in parts]
    whole = lambda n: pl.BlockSpec((TOK, n), lambda i: (0, 0))
    specs = [whole(FEATURES), whole(HD)]
    specs += [pl.BlockSpec((d, step), lambda i: (0, i)) for d in depths]
    args = [rows, inv, *parts]
    aliases = {}
    if before is not None:
        specs.append(pl.BlockSpec(memory_space=pl.ANY))
        args.append(before)
        aliases = {len(args) - 1: 0}
    columns = parts[0].shape[1]
    return pl.pallas_call(
        functools.partial(gate_kernel, depths),
        grid=(columns // step,),
        out_shape=jax.ShapeDtypeStruct((TOK, width), jnp.bfloat16),
        in_specs=specs,
        out_specs=pl.BlockSpec((TOK, step), lambda i: (0, i + first // step)),
        input_output_aliases=aliases,
        compiler_params=pltpu.CompilerParams(vmem_limit_bytes=40 << 20),
        cost_estimate=pl.CostEstimate(
            flops=2 * TOK * FEATURES * columns, bytes_accessed=2 * FEATURES * columns, transcendentals=TOK * columns
        ),
    )(*args)


def on_device(queries, keys, values, doc_lengths, shard_starts, norm_gain, ffn_weight):
    y, z, x, c = (lax.axis_index(a) for a in ("y", "z", "x", "c"))
    position = y * NZ + z
    bounds = jnp.concatenate([shard_starts, jnp.full((1,), NY * NZ * TOK, jnp.int32)])
    first = bounds[position] - position * TOK
    end = bounds[position + 1] - position * TOK
    ends = jnp.cumsum(doc_lengths)
    meta = jnp.stack([first, end, y, z, ends[0], ends[1], ends[2], ends[3], x, c]).astype(jnp.int32)
    width = ffn_weight.shape[1]

    with jax.named_scope("weight_ring"):
        ring = lax.all_gather(ffn_weight[:, :RING_COLUMNS], ("y", "z"), axis=0, tiled=True)

    with jax.named_scope("rows_to_owners"):
        up = jnp.concatenate(
            [lax.dynamic_slice_in_dim(a, TOK - first, QUARTER, 0) for a in (queries, keys, values)], axis=1
        )
        down = jnp.concatenate([a[:QUARTER] for a in (queries, keys, values)], axis=1)
        low, high = shift_cp(up, 1), shift_cp(down, -1)
        q, k, v = align(meta, queries, keys, values, low, high)

    with jax.named_scope("keys_and_values"):
        v_column = jnp.concatenate([v, shift(v, "y", 1), shift(v, "y", 2)], axis=0)
        v_all = z_ring(v_column, False).reshape(NZ, 3, TOK, HD)
        k0 = z_ring(k, False)
        k1 = shift(k0, "y", 1)
        k2 = shift(k1, "y", 1)
        k0, k1, k2 = (a.reshape(NZ, TOK, HD) for a in (k0, k1, k2))

    with jax.named_scope("weight_rows"):
        w0 = z_ring(ffn_weight[:, RING_COLUMNS:], True)
        w1 = shift(w0, "y", 1)
        w2 = shift(w0, "y", -1)
        half = w0.shape[0] // 2
        w3 = shift(w1[:half], "y", 1)
        w4 = shift(w2[half:], "y", -1)

    with jax.named_scope("attention"):
        attended = attention(meta, q, k0, k1, k2, v_all)

    with jax.named_scope("features"):
        pieces = [attended] + [shift(attended, "x", d) for d in (1, -1, 2)]
        pieces = [b for a in pieces for b in (a, shift(a, "c", 1))]
        plain, moved, inv = prepare(meta, norm_gain.reshape(1, FEATURES), pieces)

    with jax.named_scope("gate"):
        out = gate(moved, inv, [w0, w1, w2, w3, w4], None, RING_COLUMNS, width, 256)
        return gate(plain, inv, [ring], out, 0, width, 256)


def solution(mesh):
    fine = Mesh(mesh.devices.reshape(NY, NZ, NX, NC), ("y", "z", "x", "c"))
    rows, columns = ("y", "z"), ("x", "c")
    return jax.shard_map(
        on_device,
        mesh=fine,
        in_specs=(P(rows, columns), P(rows, columns), P(rows, columns), P(), P(), P(), P(rows, columns)),
        out_specs=P(rows, columns),
        check_vma=False,
    )
```

```python
import functools

import jax
import jax.numpy as jnp
from jax import lax
from jax.experimental import pallas as pl
from jax.experimental.pallas import tpu as pltpu
from jax.sharding import Mesh, PartitionSpec as P

HD = 128
TOK = 256
CAP = 384
QUARTER = TOK // 4
FEATURES = 4096
TOKENS = 8192
NY, NZ, NX, NC = 4, 8, 4, 2
HEADS_HERE = 4
HERE = 4
NEAR = 3
NORM_EPS = 1e-05
MASKED = -1e30
LOG2E = 1.4426950408889634
EXP2_SCALE = HD ** (-0.5) * LOG2E
VMEM = pl.BlockSpec(memory_space=pltpu.VMEM)
SMEM = pl.BlockSpec(memory_space=pltpu.SMEM)
ROWS, COLUMNS, TALL = ("yp", "yb", "z"), ("x", "c"), ("yp", "yb")


def shift(block, axis, distance):
    count = lax.axis_size(axis)
    return lax.ppermute(block, axis, [(i, (i + distance) % count) for i in range(count)])


def here():
    y = lax.axis_index("yp") * 2 + lax.axis_index("yb")
    return y, lax.axis_index("z"), lax.axis_index("x"), lax.axis_index("c")


def shift_both(block, across, distance):
    pairs = [(b, i) for b in range(2) for i in range(NX)]
    to = lambda b, i: (b ^ across) * NX + (i + distance) % NX
    return lax.ppermute(block, ("yb", "x"), [(b * NX + i, to(b, i)) for b, i in pairs])


def z_ring(block):
    up, down = [block], [block]
    for _ in range(3):
        up.append(shift(up[-1], "z", 1))
        down.append(shift(down[-1], "z", -1))
    near = jnp.concatenate([shift(up[3], "z", 1), up[3], up[2]], axis=0)
    return near, jnp.concatenate([up[1], block, *down[1:]], axis=0)


def bf16(*shape):
    return jax.ShapeDtypeStruct(shape, jnp.bfloat16)


def f32(*shape):
    return jax.ShapeDtypeStruct(shape, jnp.float32)


def limit(mib):
    return pltpu.CompilerParams(vmem_limit_bytes=mib << 20)


def extent(starts):
    y, z, _, _ = here()
    mine = y * NZ + z
    after = jnp.where(mine == NY * NZ - 1, TOKENS, starts[jnp.minimum(mine + 1, NY * NZ - 1)])
    return starts[mine] - mine * TOK, after - mine * TOK


def cut_kernel(starts, q, k, v, up, down):
    first, _ = extent(starts)
    row = lax.broadcasted_iota(jnp.int32, (QUARTER, CAP), 0)
    slot = lax.broadcasted_iota(jnp.int32, (QUARTER, CAP), 1)
    last = (slot == row + TOK - first).astype(jnp.bfloat16)
    at = 0
    for ref in (q, k, v):
        wide = ref.shape[1]
        up[:, at : at + wide] = jnp.dot(last, ref[...], preferred_element_type=jnp.float32).astype(jnp.bfloat16)
        down[:, at : at + wide] = ref[:QUARTER]
        at += wide


def align_kernel(starts, q, k, v, low, high, q_out, kv_out):
    first, end = extent(starts)
    row = lax.broadcasted_iota(jnp.int32, (TOK, 1), 0)
    slot = lax.broadcasted_iota(jnp.int32, (TOK, CAP), 1)
    near = lax.broadcasted_iota(jnp.int32, (TOK, QUARTER), 1)
    own = ((slot == row - first) & (row >= first) & (row < end)).astype(jnp.bfloat16)
    from_low = ((near == row) & (row < first)).astype(jnp.bfloat16)
    from_high = ((near == row - end) & (row >= end)).astype(jnp.bfloat16)
    at = 0
    for ref, out, place in ((q, q_out, 0), (k, kv_out, 0), (v, kv_out, HD)):
        wide = ref.shape[1]
        total = jnp.dot(own, ref[...], preferred_element_type=jnp.float32)
        total += jnp.dot(from_low, low[:, at : at + wide], preferred_element_type=jnp.float32)
        total += jnp.dot(from_high, high[:, at : at + wide], preferred_element_type=jnp.float32)
        out[:, place : place + wide] = total.astype(jnp.bfloat16)
        at += wide


def cut(starts, q, k, v):
    wide = q.shape[1] + k.shape[1] + v.shape[1]
    return pl.pallas_call(
        cut_kernel,
        out_shape=(bf16(QUARTER, wide),) * 2,
        in_specs=[SMEM] + [VMEM] * 3,
        out_specs=(VMEM,) * 2,
        compiler_params=limit(16),
    )(starts, q, k, v)


def align(starts, q, k, v, up, down):
    count = NY * NZ
    low = lax.ppermute(up, ROWS, [(i, (i + 1) % count) for i in range(count)])
    high = lax.ppermute(down, ROWS, [(i, (i - 1) % count) for i in range(count)])
    return pl.pallas_call(
        align_kernel,
        out_shape=(bf16(TOK, q.shape[1]), bf16(TOK, 2 * HD)),
        in_specs=[SMEM] + [VMEM] * 5,
        out_specs=(VMEM,) * 2,
        compiler_params=limit(16),
    )(starts, q, k, v, low, high)


def attention_kernel(back, parts, place, lengths, q_ref, *refs):
    blocks, refs = refs[:parts], refs[parts:]
    if back:
        old_stats, old_sums, *refs = refs
    if back == 2:
        out_ref, stats, sums = refs
    else:
        stats, sums = refs
    y, z = place() if callable(place) else place
    ends, total = [], 0
    for i in range(4):
        total += lengths[i]
        ends.append(total)
    mine = y * NZ + z
    query = mine * TOK + lax.broadcasted_iota(jnp.int32, (1, TOK), 1)

    def start_of(token):
        start = token * 0
        for end in ends:
            start = jnp.maximum(start, jnp.where(end <= token, end, 0))
        return start

    starts = start_of(query)
    lowest = start_of(mine * TOK) // TOK
    clear = (start_of(mine * TOK + TOK - 1) + TOK - 1) // TOK

    def step(ref, row, block, masked, opening):
        key, value = ref[pl.ds(row, TOK), :HD], ref[pl.ds(row, TOK), HD:]
        heads = range(HEADS_HERE)
        scores = [
            lax.dot_general(
                key, q_ref[:, h * HD : (h + 1) * HD], (((1,), (1,)), ((), ())), preferred_element_type=jnp.float32
            )
            for h in heads
        ]
        if masked:
            ids = block * TOK + lax.broadcasted_iota(jnp.int32, (TOK, 1), 0)
            allowed = (ids >= starts) & (ids <= query)
            scores = [jnp.where(allowed, s, MASKED) for s in scores]
        tops = [jnp.max(s, axis=0, keepdims=True) * EXP2_SCALE for s in scores]
        if not opening:
            was = [stats[h : h + 1] for h in heads]
            tops = [jnp.maximum(a, b) for a, b in zip(tops, was)]
            fading = [jnp.exp2(a - b) for a, b in zip(was, tops)]
        weights = [jnp.exp2(s * EXP2_SCALE - t) for s, t in zip(scores, tops)]
        mass = [jnp.sum(w, axis=0, keepdims=True) for w in weights]
        added = [
            lax.dot_general(
                value, w.astype(jnp.bfloat16), (((0,), (0,)), ((), ())), preferred_element_type=jnp.float32
            )
            for w in weights
        ]
        if not opening:
            mass = [m + stats[4 + h : 5 + h] * f for h, m, f in zip(heads, mass, fading)]
            added = [a + sums[h] * f for h, a, f in zip(heads, added, fading)]
        for h in heads:
            stats[h : h + 1] = tops[h]
            stats[4 + h : 5 + h] = mass[h]
            sums[h] = added[h]

    if back:
        stats[...] = old_stats[...]
        sums[...] = old_sums[...]
    else:
        step(blocks[1], (HERE - NEAR) * TOK, mine, True, True)
    before = 0
    for ref in blocks:

        def body(i, _, ref=ref, before=before):
            block = (y - back) * NZ + lax.rem(z + before + i - HERE + NZ, NZ)
            needed = (block >= lowest) & (block < mine)
            row = pl.multiple_of(i * TOK, TOK)

            @pl.when(needed & (block < clear))
            def _():
                step(ref, row, block, True, False)

            @pl.when(needed & (block >= clear))
            def _():
                step(ref, row, block, False, False)

            return 0

        lax.fori_loop(0, ref.shape[0] // TOK, body, 0)
        before += ref.shape[0] // TOK
    if back == 2:
        for h in range(HEADS_HERE):
            out_ref[:, h * HD : (h + 1) * HD] = (sums[h] / stats[4 + h : 5 + h]).T.astype(jnp.bfloat16)


def attention(back, lengths, q, blocks, state, place=lambda: here()[:2]):
    shapes = [f32(2 * HEADS_HERE, TOK), f32(HEADS_HERE, HD, TOK)]
    kwargs = {}
    if back == 2:
        kwargs["scratch_shapes"] = [pltpu.VMEM(s.shape, s.dtype) for s in shapes]
        shapes = [bf16(TOK, HEADS_HERE * HD)]
    work = 8 * HEADS_HERE * TOK * TOK
    return pl.pallas_call(
        functools.partial(attention_kernel, back, len(blocks), place),
        out_shape=tuple(shapes),
        in_specs=[SMEM] + [VMEM] * (1 + len(blocks) + len(state)),
        out_specs=(VMEM,) * len(shapes),
        compiler_params=limit(32),
        cost_estimate=pl.CostEstimate(flops=4 * work * HD, bytes_accessed=4 << 20, transcendentals=work),
        **kwargs,
    )(lengths, q, *blocks, *state)


def gate_kernel(gain, mine, other, weight, out, rows):
    y, _, x, c = here()
    squares = jnp.zeros((TOK, HD), jnp.float32)
    for side, pieces in enumerate((mine, other)):
        for i in range(NX):
            tp = lax.rem(x + (0, 3, 1, 2)[i], NX) * NC + (c if side == 0 else 1 - c)
            for j in range(HEADS_HERE):
                head = tp * HEADS_HERE + j
                part = pieces[i * TOK : (i + 1) * TOK, j * HD : (j + 1) * HD].astype(jnp.float32)
                squares += part * part
                scaled = (part * gain[:, pl.ds(pl.multiple_of(head * HD, HD), HD)]).astype(jnp.bfloat16)
                away = lax.rem(head // NZ - y + NY, NY)
                slot = jnp.where(away == 0, 0, jnp.where(away == 3, 1, away + 1))
                place = lax.rem(head, NZ) * NY + slot
                rows[:, pl.ds(pl.multiple_of(place * HD, HD), HD)] = scaled
    inv = lax.rsqrt(jnp.sum(squares, axis=1, keepdims=True) / FEATURES + NORM_EPS)

    def columns(i, _):
        at = pl.ds(pl.multiple_of(i * HD, HD), HD)
        value = jnp.dot(rows[...], weight[:, at], preferred_element_type=jnp.float32) * inv
        out[:, at] = (value / (1.0 + jnp.exp(-value))).astype(jnp.bfloat16)
        return 0

    lax.fori_loop(0, out.shape[1] // HD, columns, 0)


def gate(gain, mine, other, weight):
    columns = weight.shape[1]
    return pl.pallas_call(
        gate_kernel,
        out_shape=bf16(TOK, columns),
        in_specs=[VMEM] * 4,
        out_specs=VMEM,
        scratch_shapes=[pltpu.VMEM((TOK, FEATURES), jnp.bfloat16)],
        compiler_params=limit(24),
        cost_estimate=pl.CostEstimate(
            flops=2 * TOK * FEATURES * columns, bytes_accessed=2 * FEATURES * columns, transcendentals=TOK * columns
        ),
    )(gain, mine, other, weight)


def join_kernel(home, back, out):
    columns = home.shape[1]
    odd = lax.rem(here()[0], 2)
    out[:, pl.ds(pl.multiple_of(odd * columns, HD), columns)] = home[...]
    out[:, pl.ds(pl.multiple_of((1 - odd) * columns, HD), columns)] = back[...]


def join(home, back):
    return pl.pallas_call(
        join_kernel,
        out_shape=bf16(TOK, 2 * home.shape[1]),
        in_specs=[VMEM] * 2,
        out_specs=VMEM,
        compiler_params=limit(8),
    )(home, back)


def on_device(queries, keys, values, doc_lengths, shard_starts, norm_gain, ffn_weight):
    half = ffn_weight.shape[1] // 2
    odd = lax.axis_index("yb") == 1

    with jax.named_scope("rows_to_owners"):
        up, down = cut(shard_starts, queries, keys, values)
        odd, up, down = lax.optimization_barrier((odd, up, down))
        q, kv = align(shard_starts, queries, keys, values, up, down)

    with jax.named_scope("weight_rows"):
        left, right = ffn_weight[:, :half], ffn_weight[:, half:]
        theirs, mine = jnp.where(odd, left, right), jnp.where(odd, right, left)
        parts = [mine, shift(theirs, TALL, 1), shift(theirs, TALL, -1), shift(mine, TALL, 2)]
        *parts, kv = lax.optimization_barrier((*parts, kv))
        weight = lax.all_gather(jnp.concatenate(parts, axis=0), "z", axis=0, tiled=True)

    with jax.named_scope("keys_and_values"):
        near, far = z_ring(kv)
        near1, far3 = shift(near, TALL, 1), shift(far, TALL, -1)
        far1 = shift(far, TALL, 1)
        near2, far2 = shift(near1, TALL, 1), shift(far3, TALL, -1)

    with jax.named_scope("attention"):
        state = attention(0, doc_lengths, q, [near, far], ())
        state = attention(1, doc_lengths, q, [near1, far1], state)
        (attended,) = attention(2, doc_lengths, q, [near2, far2], state)

    gain = norm_gain.reshape(1, FEATURES)
    with jax.named_scope("features_of_the_pair"):
        pieces = [shift_both(attended, 1, d) for d in (0, 1, -1, 2)]
        own = [attended] + [shift(attended, "x", d) for d in (1, -1, 2)]
        mine = jnp.concatenate(pieces, axis=0)
        away = gate(gain, mine, shift(mine, "c", 1), weight)

    with jax.named_scope("features"):
        *own, away = lax.optimization_barrier((*own, away))
        mine = jnp.concatenate(own, axis=0)
        home = gate(gain, mine, shift(mine, "c", 1), weight)
        return join(home, shift(away, "yb", 1))


def solution(mesh):
    fine = Mesh(mesh.devices.reshape(NY // 2, 2, NZ, NX, NC), ("yp", "yb", "z", "x", "c"))
    return jax.shard_map(
        on_device,
        mesh=fine,
        in_specs=(P(ROWS, COLUMNS), P(ROWS, COLUMNS), P(ROWS, COLUMNS), P(), P(), P(), P(ROWS, COLUMNS)),
        out_specs=P(ROWS, COLUMNS),
        check_vma=False,
    )
```

```python
import functools

import jax
import jax.numpy as jnp
from jax import lax
from jax.experimental import pallas as pl
from jax.experimental.pallas import tpu as pltpu
from jax.sharding import Mesh, PartitionSpec as P

HD = 128
TOK = 256
CAP = 384
QUARTER = TOK // 4
FEATURES = 4096
TOKENS = 8192
NY, NZ, NX, NC = 4, 8, 4, 2
HEADS_HERE = 4
HERE = 2
FAR = 5
PARTS = 4
NORM_EPS = 1e-05
MASKED = -1e30
LOG2E = 1.4426950408889634
EXP2_SCALE = HD ** (-0.5) * LOG2E
VMEM = pl.BlockSpec(memory_space=pltpu.VMEM)
HBM = pl.BlockSpec(memory_space=pltpu.HBM)
SMEM = pl.BlockSpec(memory_space=pltpu.SMEM)
ROWS, COLUMNS, TALL = ("yp", "yb", "z"), ("x", "c"), ("yp", "yb")


def shift(block, axis, distance):
    count = lax.axis_size(axis)
    return lax.ppermute(block, axis, [(i, (i + distance) % count) for i in range(count)])


def here():
    y = lax.axis_index("yp") * 2 + lax.axis_index("yb")
    return y, lax.axis_index("z"), lax.axis_index("x"), lax.axis_index("c")


def shift_both(block, across, distance):
    pairs = [(b, i) for b in range(2) for i in range(NX)]
    to = lambda b, i: (b ^ across) * NX + (i + distance) % NX
    return lax.ppermute(block, ("yb", "x"), [(b * NX + i, to(b, i)) for b, i in pairs])


def z_blocks(block):
    up1, down1, up2, down2 = (shift(block, "z", d) for d in (1, -1, 2, -2))
    far = jnp.concatenate([up2, up1, block, down1, down2], axis=0)
    up2, down2, far = lax.optimization_barrier((up2, down2, far))
    return far, jnp.concatenate([shift(down2, "z", -1), shift(up2, "z", 2), shift(up2, "z", 1)], axis=0)


def bf16(*shape):
    return jax.ShapeDtypeStruct(shape, jnp.bfloat16)


def f32(*shape):
    return jax.ShapeDtypeStruct(shape, jnp.float32)


def limit(mib):
    return pltpu.CompilerParams(vmem_limit_bytes=mib << 20)


def extent(starts):
    y, z, _, _ = here()
    mine = y * NZ + z
    after = jnp.where(mine == NY * NZ - 1, TOKENS, starts[jnp.minimum(mine + 1, NY * NZ - 1)])
    return starts[mine] - mine * TOK, after - mine * TOK


def open_kernel(starts, q, k, v, weight, up, down, theirs, mine, last, sems):
    first, _ = extent(starts)
    half, odd = weight.shape[1] // 2, lax.rem(here()[0], 2)
    column = lambda side: weight.at[:, pl.ds(pl.multiple_of(side * half, HD), half)]
    pairs = [(column(1 - odd), theirs), (column(odd), mine)]
    at, ends = 0, []
    for ref in (q, k, v):
        wide = ref.shape[1]
        pairs.append((ref.at[pl.ds(0, QUARTER)], down.at[:, pl.ds(at, wide)]))
        pairs.append((ref.at[pl.ds(CAP - 3 * QUARTER, 3 * QUARTER)], last.at[:, pl.ds(at, wide)]))
        at += wide
    copies = [pltpu.make_async_copy(a, b, sems.at[i]) for i, (a, b) in enumerate(pairs)]
    for copy in copies:
        copy.start()
    for copy in copies:
        copy.wait()
    row = lax.broadcasted_iota(jnp.int32, (QUARTER, 3 * QUARTER), 0)
    slot = lax.broadcasted_iota(jnp.int32, (QUARTER, 3 * QUARTER), 1) + CAP - 3 * QUARTER
    picked = (slot == row + TOK - first).astype(jnp.bfloat16)
    up[...] = jnp.dot(picked, last[...], preferred_element_type=jnp.float32).astype(jnp.bfloat16)


def align_kernel(starts, q, k, v, low, high, q_out, kv_out):
    first, end = extent(starts)
    row = lax.broadcasted_iota(jnp.int32, (TOK, 1), 0)
    slot = lax.broadcasted_iota(jnp.int32, (TOK, CAP), 1)
    near = lax.broadcasted_iota(jnp.int32, (TOK, QUARTER), 1)
    own = ((slot == row - first) & (row >= first) & (row < end)).astype(jnp.bfloat16)
    from_low = ((near == row) & (row < first)).astype(jnp.bfloat16)
    from_high = ((near == row - end) & (row >= end)).astype(jnp.bfloat16)
    at = 0
    for ref, out, place in ((q, q_out, 0), (k, kv_out, 0), (v, kv_out, HD)):
        wide = ref.shape[1]
        total = jnp.dot(own, ref[...], preferred_element_type=jnp.float32)
        total += jnp.dot(from_low, low[:, at : at + wide], preferred_element_type=jnp.float32)
        total += jnp.dot(from_high, high[:, at : at + wide], preferred_element_type=jnp.float32)
        out[:, place : place + wide] = total.astype(jnp.bfloat16)
        at += wide


def opening(starts, q, k, v, weight):
    wide = q.shape[1] + k.shape[1] + v.shape[1]
    rows, half = weight.shape[0], weight.shape[1] // 2
    return pl.pallas_call(
        open_kernel,
        out_shape=(bf16(QUARTER, wide),) * 2 + (bf16(rows, half),) * 2,
        in_specs=[SMEM] + [HBM] * 4,
        out_specs=(VMEM,) * 4,
        scratch_shapes=[pltpu.VMEM((3 * QUARTER, wide), jnp.bfloat16), pltpu.SemaphoreType.DMA((8,))],
        compiler_params=limit(60),
    )(starts, q, k, v, weight)


def align(starts, q, k, v, up, down):
    count = NY * NZ
    low = lax.ppermute(up, ROWS, [(i, (i + 1) % count) for i in range(count)])
    high = lax.ppermute(down, ROWS, [(i, (i - 1) % count) for i in range(count)])
    return pl.pallas_call(
        align_kernel,
        out_shape=(bf16(TOK, q.shape[1]), bf16(TOK, 2 * HD)),
        in_specs=[SMEM] + [VMEM] * 5,
        out_specs=(VMEM,) * 2,
        compiler_params=limit(60),
    )(starts, q, k, v, low, high)


def attention_kernel(back, parts, place, lengths, q_ref, *refs):
    blocks, refs = refs[:parts], refs[parts:]
    if back:
        old_stats, old_sums, *refs = refs
    if back == 2:
        out_ref, stats, sums = refs
    else:
        stats, sums = refs
    y, z = place() if callable(place) else place
    ends, total = [], 0
    for i in range(4):
        total += lengths[i]
        ends.append(total)
    mine = y * NZ + z
    query = mine * TOK + lax.broadcasted_iota(jnp.int32, (1, TOK), 1)

    def start_of(token):
        start = token * 0
        for end in ends:
            start = jnp.maximum(start, jnp.where(end <= token, end, 0))
        return start

    starts = start_of(query)
    lowest = start_of(mine * TOK) // TOK
    clear = (start_of(mine * TOK + TOK - 1) + TOK - 1) // TOK

    def step(ref, row, block, masked, opening):
        key, value = ref[pl.ds(row, TOK), :HD], ref[pl.ds(row, TOK), HD:]
        heads = range(HEADS_HERE)
        scores = [
            lax.dot_general(
                key, q_ref[:, h * HD : (h + 1) * HD], (((1,), (1,)), ((), ())), preferred_element_type=jnp.float32
            )
            for h in heads
        ]
        if masked:
            ids = block * TOK + lax.broadcasted_iota(jnp.int32, (TOK, 1), 0)
            allowed = (ids >= starts) & (ids <= query)
            scores = [jnp.where(allowed, s, MASKED) for s in scores]
        tops = [jnp.max(s, axis=0, keepdims=True) * EXP2_SCALE for s in scores]
        if not opening:
            was = [stats[h : h + 1] for h in heads]
            tops = [jnp.maximum(a, b) for a, b in zip(tops, was)]
            fading = [jnp.exp2(a - b) for a, b in zip(was, tops)]
        weights = [jnp.exp2(s * EXP2_SCALE - t) for s, t in zip(scores, tops)]
        mass = [jnp.sum(w, axis=0, keepdims=True) for w in weights]
        added = [
            lax.dot_general(
                value, w.astype(jnp.bfloat16), (((0,), (0,)), ((), ())), preferred_element_type=jnp.float32
            )
            for w in weights
        ]
        if not opening:
            mass = [m + stats[4 + h : 5 + h] * f for h, m, f in zip(heads, mass, fading)]
            added = [a + sums[h] * f for h, a, f in zip(heads, added, fading)]
        for h in heads:
            stats[h : h + 1] = tops[h]
            stats[4 + h : 5 + h] = mass[h]
            sums[h] = added[h]

    if back:
        stats[...] = old_stats[...]
        sums[...] = old_sums[...]
    else:
        step(blocks[0], HERE * TOK, mine, True, True)
    before = 0
    for ref in blocks:

        def body(i, _, ref=ref, before=before):
            block = (y - back) * NZ + lax.rem(z + before + i - HERE + NZ, NZ)
            needed = (block >= lowest) & (block < mine)
            row = pl.multiple_of(i * TOK, TOK)

            @pl.when(needed & (block < clear))
            def _():
                step(ref, row, block, True, False)

            @pl.when(needed & (block >= clear))
            def _():
                step(ref, row, block, False, False)

            return 0

        lax.fori_loop(0, ref.shape[0] // TOK, body, 0)
        before += ref.shape[0] // TOK
    if back == 2:
        for h in range(HEADS_HERE):
            out_ref[:, h * HD : (h + 1) * HD] = (sums[h] / stats[4 + h : 5 + h]).T.astype(jnp.bfloat16)


def attention(back, lengths, q, blocks, state, place=lambda: here()[:2]):
    shapes = [f32(2 * HEADS_HERE, TOK), f32(HEADS_HERE, HD, TOK)]
    kwargs = {}
    if back == 2:
        kwargs["scratch_shapes"] = [pltpu.VMEM(s.shape, s.dtype) for s in shapes]
        shapes = [bf16(TOK, HEADS_HERE * HD)]
    work = 8 * HEADS_HERE * TOK * TOK
    return pl.pallas_call(
        functools.partial(attention_kernel, back, len(blocks), place),
        out_shape=tuple(shapes),
        in_specs=[SMEM] + [VMEM] * (1 + len(blocks) + len(state)),
        out_specs=(VMEM,) * len(shapes),
        compiler_params=limit(32),
        cost_estimate=pl.CostEstimate(flops=4 * work * HD, bytes_accessed=4 << 20, transcendentals=work),
        **kwargs,
    )(lengths, q, *blocks, *state)


def gate_kernel(gain, mine, other, weight, out, rows, held, total, sems):
    depth = FEATURES // PARTS
    parts = [pl.ds(i * depth, depth) for i in range(PARTS)]
    copies = [pltpu.make_async_copy(weight.at[p], held.at[p], sems.at[i]) for i, p in enumerate(parts)]
    for copy in copies:
        copy.start()
    y, _, x, c = here()
    squares = jnp.zeros((TOK, HD), jnp.float32)
    for side, pieces in enumerate((mine, other)):
        for i in range(NX):
            tp = lax.rem(x + (0, 3, 1, 2)[i], NX) * NC + (c if side == 0 else 1 - c)
            for j in range(HEADS_HERE):
                head = tp * HEADS_HERE + j
                part = pieces[i * TOK : (i + 1) * TOK, j * HD : (j + 1) * HD].astype(jnp.float32)
                squares += part * part
                scaled = (part * gain[:, pl.ds(pl.multiple_of(head * HD, HD), HD)]).astype(jnp.bfloat16)
                away = lax.rem(head // NZ - y + NY, NY)
                slot = jnp.where(away == 0, 0, jnp.where(away == 3, 1, away + 1))
                place = lax.rem(head, NZ) * NY + slot
                rows[:, pl.ds(pl.multiple_of(place * HD, HD), HD)] = scaled
    inv = lax.rsqrt(jnp.sum(squares, axis=1, keepdims=True) / FEATURES + NORM_EPS)
    for i, copy in enumerate(copies):
        copy.wait()
        term = jnp.dot(
            rows[:, i * depth : (i + 1) * depth],
            held[i * depth : (i + 1) * depth],
            preferred_element_type=jnp.float32,
        )
        if i == 0:
            total[...] = term
        elif i < PARTS - 1:
            total[...] += term
        else:
            value = (total[...] + term) * inv
            out[...] = (value / (1.0 + jnp.exp(-value))).astype(jnp.bfloat16)


def gate(gain, mine, other, weight):
    columns = weight.shape[1]
    return pl.pallas_call(
        gate_kernel,
        out_shape=bf16(TOK, columns),
        in_specs=[VMEM] * 3 + [HBM],
        out_specs=VMEM,
        scratch_shapes=[
            pltpu.VMEM((TOK, FEATURES), jnp.bfloat16),
            pltpu.VMEM(weight.shape, weight.dtype),
            pltpu.VMEM((TOK, columns), jnp.float32),
            pltpu.SemaphoreType.DMA((PARTS,)),
        ],
        compiler_params=limit(28),
        cost_estimate=pl.CostEstimate(
            flops=2 * TOK * FEATURES * columns, bytes_accessed=2 * FEATURES * columns, transcendentals=TOK * columns
        ),
    )(gain, mine, other, pltpu.with_memory_space_constraint(weight, pltpu.HBM))


def join_kernel(home, back, out):
    columns = home.shape[1]
    odd = lax.rem(here()[0], 2)
    out[:, pl.ds(pl.multiple_of(odd * columns, HD), columns)] = home[...]
    out[:, pl.ds(pl.multiple_of((1 - odd) * columns, HD), columns)] = back[...]


def join(home, back):
    return pl.pallas_call(
        join_kernel,
        out_shape=bf16(TOK, 2 * home.shape[1]),
        in_specs=[VMEM] * 2,
        out_specs=VMEM,
        compiler_params=limit(8),
    )(home, back)


def on_device(queries, keys, values, doc_lengths, shard_starts, norm_gain, ffn_weight):
    with jax.named_scope("rows_to_owners"):
        up, down, theirs, mine = opening(shard_starts, queries, keys, values, ffn_weight)
        q, kv = align(shard_starts, queries, keys, values, up, down)

    with jax.named_scope("weight_rows"):
        parts = [mine, shift(theirs, TALL, 1), shift(theirs, TALL, -1), shift(mine, TALL, 2)]
        *parts, kv = lax.optimization_barrier((*parts, kv))
        weight = lax.all_gather(jnp.concatenate(parts, axis=0), "z", axis=0, tiled=True)

    with jax.named_scope("keys_and_values"):
        far, near = z_blocks(kv)
        far1, far3 = shift(far, TALL, 1), shift(far, TALL, -1)
        near1, far2 = shift(near, TALL, 1), shift(far3, TALL, -1)
        state = attention(0, doc_lengths, q, [far, near], ())
        near1, far1, *state = lax.optimization_barrier((near1, far1, *state))
        near2 = shift(near1, TALL, 1)

    with jax.named_scope("attention"):
        state = attention(1, doc_lengths, q, [far1, near1], state)
        (attended,) = attention(2, doc_lengths, q, [far2, near2], state)

    gain = norm_gain.reshape(1, FEATURES)
    with jax.named_scope("features_of_the_pair"):
        pieces = [shift_both(attended, 1, d) for d in (0, 1, -1, 2)]
        own = [attended] + [shift(attended, "x", d) for d in (1, -1, 2)]
        mine = jnp.concatenate(pieces, axis=0)
        away = gate(gain, mine, shift(mine, "c", 1), weight)

    with jax.named_scope("features"):
        *own, away = lax.optimization_barrier((*own, away))
        mine = jnp.concatenate(own, axis=0)
        home = gate(gain, mine, shift(mine, "c", 1), weight)
        return join(home, shift(away, "yb", 1))


def solution(mesh):
    fine = Mesh(mesh.devices.reshape(NY // 2, 2, NZ, NX, NC), ("yp", "yb", "z", "x", "c"))
    return jax.shard_map(
        on_device,
        mesh=fine,
        in_specs=(P(ROWS, COLUMNS), P(ROWS, COLUMNS), P(ROWS, COLUMNS), P(), P(), P(), P(ROWS, COLUMNS)),
        out_specs=P(ROWS, COLUMNS),
        check_vma=False,
    )
```

```python
import functools

import jax
import jax.numpy as jnp
from jax import lax
from jax.experimental import pallas as pl
from jax.experimental.pallas import tpu as pltpu
from jax.sharding import Mesh, PartitionSpec as P

HD = 128
TOK = 256
CAP = 384
QUARTER = TOK // 4
FEATURES = 4096
TOKENS = 8192
NY, NZ, NX, NC = 4, 8, 4, 2
HEADS_HERE = 4
HERE = 2
FAR = 5
SENT_FIRST = 512
PARTS = 4
NORM_EPS = 1e-05
MASKED = -1e30
LOG2E = 1.4426950408889634
EXP2_SCALE = HD ** (-0.5) * LOG2E
VMEM = pl.BlockSpec(memory_space=pltpu.VMEM)
HBM = pl.BlockSpec(memory_space=pltpu.HBM)
SMEM = pl.BlockSpec(memory_space=pltpu.SMEM)
ROWS, COLUMNS, TALL = ("yp", "yb", "z"), ("x", "c"), ("yp", "yb")


def shift(block, axis, distance):
    count = lax.axis_size(axis)
    return lax.ppermute(block, axis, [(i, (i + distance) % count) for i in range(count)])


def here():
    y = lax.axis_index("yp") * 2 + lax.axis_index("yb")
    return y, lax.axis_index("z"), lax.axis_index("x"), lax.axis_index("c")


def hop(block, *route, below=NZ):
    return lax.ppermute(block, ROWS, [(a * NZ + z, b * NZ + z) for a, b in route for z in range(below)])


def shift_both(block, across, distance):
    pairs = [(b, i) for b in range(2) for i in range(NX)]
    to = lambda b, i: (b ^ across) * NX + (i + distance) % NX
    return lax.ppermute(block, ("yb", "x"), [(b * NX + i, to(b, i)) for b, i in pairs])


def z_blocks(block):
    up1, down1 = shift(block, "z", 1), shift(block, "z", -1)
    up2, down2 = shift(up1, "z", 1), shift(down1, "z", -1)
    far = jnp.concatenate([up2, up1, block, down1, down2], axis=0)
    up2, down2, far = lax.optimization_barrier((up2, down2, far))
    return far, jnp.concatenate([shift(down2, "z", -1), shift(up2, "z", 2), shift(up2, "z", 1)], axis=0)


def bf16(*shape):
    return jax.ShapeDtypeStruct(shape, jnp.bfloat16)


def f32(*shape):
    return jax.ShapeDtypeStruct(shape, jnp.float32)


def limit(mib):
    return pltpu.CompilerParams(vmem_limit_bytes=mib << 20)


def extent(starts):
    y, z, _, _ = here()
    mine = y * NZ + z
    after = jnp.where(mine == NY * NZ - 1, TOKENS, starts[jnp.minimum(mine + 1, NY * NZ - 1)])
    return starts[mine] - mine * TOK, after - mine * TOK


def open_kernel(starts, q, k, v, weight, own, up, down, theirs, mine, sems):
    first, _ = extent(starts)
    half, odd = weight.shape[1] // 2, lax.rem(here()[0], 2)
    column = lambda side: weight.at[:, pl.ds(pl.multiple_of(side * half, HD), half)]
    at, pairs = 0, []
    for ref in (q, k, v):
        pairs.append((ref, own.at[:, pl.ds(at, ref.shape[1])]))
        at += ref.shape[1]
    pairs += [(column(1 - odd), theirs), (column(odd), mine)]
    copies = [pltpu.make_async_copy(a, b, sems.at[i]) for i, (a, b) in enumerate(pairs)]
    for copy in copies:
        copy.start()
    for copy in copies:
        copy.wait()
    row = lax.broadcasted_iota(jnp.int32, (QUARTER, CAP), 0)
    slot = lax.broadcasted_iota(jnp.int32, (QUARTER, CAP), 1)
    picked = (slot == row + TOK - first).astype(jnp.bfloat16)
    up[...] = jnp.dot(picked, own[...], preferred_element_type=jnp.float32).astype(jnp.bfloat16)
    down[...] = own[:QUARTER]


def align_kernel(starts, rows, low, high, own_part, below, above, far_part, q_out, kv_out, pair, sems):
    depth = own_part.shape[0]
    copies = [
        pltpu.make_async_copy(part, pair.at[pl.ds(i * depth, depth)], sems.at[i])
        for i, part in enumerate((own_part, below, above, far_part))
    ]
    for copy in copies:
        copy.start()
    first, end = extent(starts)
    row = lax.broadcasted_iota(jnp.int32, (TOK, 1), 0)
    slot = lax.broadcasted_iota(jnp.int32, (TOK, CAP), 1)
    near = lax.broadcasted_iota(jnp.int32, (TOK, QUARTER), 1)
    own = ((slot == row - first) & (row >= first) & (row < end)).astype(jnp.bfloat16)
    from_low = ((near == row) & (row < first)).astype(jnp.bfloat16)
    from_high = ((near == row - end) & (row >= end)).astype(jnp.bfloat16)
    total = jnp.dot(own, rows[...], preferred_element_type=jnp.float32)
    total += jnp.dot(from_low, low[...], preferred_element_type=jnp.float32)
    total += jnp.dot(from_high, high[...], preferred_element_type=jnp.float32)
    wide = q_out.shape[1]
    q_out[...] = total[:, :wide].astype(jnp.bfloat16)
    kv_out[...] = total[:, wide:].astype(jnp.bfloat16)
    for copy in copies:
        copy.wait()


def in_hbm(array):
    return pltpu.with_memory_space_constraint(array, pltpu.HBM)


def opening(starts, q, k, v, weight):
    wide = q.shape[1] + k.shape[1] + v.shape[1]
    rows, half = weight.shape[0], weight.shape[1] // 2
    return pl.pallas_call(
        open_kernel,
        out_shape=(bf16(CAP, wide), *(bf16(QUARTER, wide),) * 2, *(bf16(rows, half),) * 2),
        in_specs=[SMEM] + [HBM] * 4,
        out_specs=(VMEM,) * 5,
        scratch_shapes=[pltpu.SemaphoreType.DMA((5,))],
        compiler_params=limit(16),
    )(starts, *(in_hbm(a) for a in (q, k, v, weight)))


def align(starts, own, up, down, parts):
    count = NY * NZ
    low = lax.ppermute(up, ROWS, [(i, (i + 1) % count) for i in range(count)])
    high = lax.ppermute(down, ROWS, [(i, (i - 1) % count) for i in range(count)])
    depth, columns = parts[0].shape
    return pl.pallas_call(
        align_kernel,
        out_shape=(bf16(TOK, HEADS_HERE * HD), bf16(TOK, 2 * HD), bf16(NY * depth, columns)),
        in_specs=[SMEM] + [VMEM] * 7,
        out_specs=(VMEM, VMEM, HBM),
        scratch_shapes=[pltpu.SemaphoreType.DMA((4,))],
        compiler_params=limit(16),
    )(starts, own, low, high, *parts)


def attention_kernel(back, parts, place, lengths, q_ref, *refs):
    blocks, refs = refs[:parts], refs[parts:]
    if back:
        old_stats, old_sums, *refs = refs
    if back == 2:
        out_ref, stats, sums = refs
    else:
        stats, sums = refs
    y, z = place() if callable(place) else place
    ends, total = [], 0
    for i in range(4):
        total += lengths[i]
        ends.append(total)
    mine = y * NZ + z
    query = mine * TOK + lax.broadcasted_iota(jnp.int32, (1, TOK), 1)

    def start_of(token):
        start = token * 0
        for end in ends:
            start = jnp.maximum(start, jnp.where(end <= token, end, 0))
        return start

    starts = start_of(query)
    lowest = start_of(mine * TOK) // TOK
    clear = (start_of(mine * TOK + TOK - 1) + TOK - 1) // TOK

    def step(ref, row, block, masked, opening):
        key, value = ref[pl.ds(row, TOK), :HD], ref[pl.ds(row, TOK), HD:]
        heads = range(HEADS_HERE)
        scores = [
            lax.dot_general(
                key, q_ref[:, h * HD : (h + 1) * HD], (((1,), (1,)), ((), ())), preferred_element_type=jnp.float32
            )
            for h in heads
        ]
        if masked:
            ids = block * TOK + lax.broadcasted_iota(jnp.int32, (TOK, 1), 0)
            allowed = (ids >= starts) & (ids <= query)
            scores = [jnp.where(allowed, s, MASKED) for s in scores]
        tops = [jnp.max(s, axis=0, keepdims=True) * EXP2_SCALE for s in scores]
        if not opening:
            was = [stats[h : h + 1] for h in heads]
            tops = [jnp.maximum(a, b) for a, b in zip(tops, was)]
            fading = [jnp.exp2(a - b) for a, b in zip(was, tops)]
        weights = [jnp.exp2(s * EXP2_SCALE - t) for s, t in zip(scores, tops)]
        mass = [jnp.sum(w, axis=0, keepdims=True) for w in weights]
        added = [
            lax.dot_general(
                value, w.astype(jnp.bfloat16), (((0,), (0,)), ((), ())), preferred_element_type=jnp.float32
            )
            for w in weights
        ]
        if not opening:
            mass = [m + stats[4 + h : 5 + h] * f for h, m, f in zip(heads, mass, fading)]
            added = [a + sums[h] * f for h, a, f in zip(heads, added, fading)]
        for h in heads:
            stats[h : h + 1] = tops[h]
            stats[4 + h : 5 + h] = mass[h]
            sums[h] = added[h]

    if back:
        stats[...] = old_stats[...]
        sums[...] = old_sums[...]
    else:
        step(blocks[0], HERE * TOK, mine, True, True)
    before = 0
    for ref in blocks:

        def body(i, _, ref=ref, before=before):
            block = (y - back) * NZ + lax.rem(z + before + i - HERE + NZ, NZ)
            needed = (block >= lowest) & (block < mine)
            row = pl.multiple_of(i * TOK, TOK)

            @pl.when(needed & (block < clear))
            def _():
                step(ref, row, block, True, False)

            @pl.when(needed & (block >= clear))
            def _():
                step(ref, row, block, False, False)

            return 0

        lax.fori_loop(0, ref.shape[0] // TOK, body, 0)
        before += ref.shape[0] // TOK
    if back == 2:
        for h in range(HEADS_HERE):
            out_ref[:, h * HD : (h + 1) * HD] = (sums[h] / stats[4 + h : 5 + h]).T.astype(jnp.bfloat16)


def attention(back, lengths, q, blocks, state, place=lambda: here()[:2]):
    shapes = [f32(2 * HEADS_HERE, TOK), f32(HEADS_HERE, HD, TOK)]
    kwargs = {}
    if back == 2:
        kwargs["scratch_shapes"] = [pltpu.VMEM(s.shape, s.dtype) for s in shapes]
        shapes = [bf16(TOK, HEADS_HERE * HD)]
    work = 8 * HEADS_HERE * TOK * TOK
    return pl.pallas_call(
        functools.partial(attention_kernel, back, len(blocks), place),
        out_shape=tuple(shapes),
        in_specs=[SMEM] + [VMEM] * (1 + len(blocks) + len(state)),
        out_specs=(VMEM,) * len(shapes),
        compiler_params=limit(32),
        cost_estimate=pl.CostEstimate(flops=4 * work * HD, bytes_accessed=4 << 20, transcendentals=work),
        **kwargs,
    )(lengths, q, *blocks, *state)


def prepare_kernel(gain, mine, other, rows, inv):
    y, _, x, c = here()
    squares = jnp.zeros((TOK, HD), jnp.float32)
    for side, pieces in enumerate((mine, other)):
        for i in range(NX):
            tp = lax.rem(x + (0, 3, 1, 2)[i], NX) * NC + (c if side == 0 else 1 - c)
            for j in range(HEADS_HERE):
                head = tp * HEADS_HERE + j
                part = pieces[i * TOK : (i + 1) * TOK, j * HD : (j + 1) * HD].astype(jnp.float32)
                squares += part * part
                scaled = (part * gain[:, pl.ds(pl.multiple_of(head * HD, HD), HD)]).astype(jnp.bfloat16)
                away = lax.rem(head // NZ - y + NY, NY)
                slot = jnp.where(away == 0, 0, jnp.where(away == 3, 1, away + 1))
                place = lax.rem(head, NZ) * NY + slot
                rows[:, pl.ds(pl.multiple_of(place * HD, HD), HD)] = scaled
    mean = jnp.sum(squares, axis=1, keepdims=True) / FEATURES
    inv[...] = jnp.broadcast_to(lax.rsqrt(mean + NORM_EPS), (TOK, HD))


def prepare(gain, mine, other):
    return pl.pallas_call(
        prepare_kernel,
        out_shape=(bf16(TOK, FEATURES), f32(TOK, HD)),
        in_specs=[VMEM] * 3,
        out_specs=(VMEM,) * 2,
        compiler_params=limit(16),
    )(gain, mine, other)


def gate_kernel(first, rows, inv, weight, out, held, total, sems):
    depth = FEATURES // PARTS
    parts = [pl.ds(i * depth, depth) for i in range(PARTS)]
    columns = pl.ds(first, out.shape[1])
    copies = [pltpu.make_async_copy(weight.at[p, columns], held.at[p], sems.at[i]) for i, p in enumerate(parts)]
    for copy in copies:
        copy.start()
    for i, copy in enumerate(copies):
        copy.wait()
        term = jnp.dot(
            rows[:, i * depth : (i + 1) * depth],
            held[i * depth : (i + 1) * depth],
            preferred_element_type=jnp.float32,
        )
        if i == 0:
            total[...] = term
        elif i < PARTS - 1:
            total[...] += term
        else:
            value = (total[...] + term) * inv[:, :1]
            out[...] = (value / (1.0 + jnp.exp(-value))).astype(jnp.bfloat16)


def gate(rows, inv, weight, first, columns):
    return pl.pallas_call(
        functools.partial(gate_kernel, first),
        out_shape=bf16(TOK, columns),
        in_specs=[VMEM] * 2 + [HBM],
        out_specs=VMEM,
        scratch_shapes=[
            pltpu.VMEM((FEATURES, columns), weight.dtype),
            pltpu.VMEM((TOK, columns), jnp.float32),
            pltpu.SemaphoreType.DMA((PARTS,)),
        ],
        compiler_params=limit(28),
        cost_estimate=pl.CostEstimate(
            flops=2 * TOK * FEATURES * columns, bytes_accessed=2 * FEATURES * columns, transcendentals=TOK * columns
        ),
    )(rows, inv, in_hbm(weight))


def join_kernel(*refs):
    *parts, out = refs
    half, odd = out.shape[1] // 2, lax.rem(here()[0], 2)
    at = 0
    for ref in parts:
        side = odd if at < half else 1 - odd
        place = side * half + at % half
        out[:, pl.ds(pl.multiple_of(place, HD), ref.shape[1])] = ref[...]
        at += ref.shape[1]


def join(*parts):
    return pl.pallas_call(
        join_kernel,
        out_shape=bf16(TOK, sum(part.shape[1] for part in parts)),
        in_specs=[VMEM] * len(parts),
        out_specs=VMEM,
        compiler_params=limit(8),
    )(*parts)


def on_device(queries, keys, values, doc_lengths, shard_starts, norm_gain, ffn_weight):
    with jax.named_scope("rows_to_owners"):
        own, up, down, theirs, mine = opening(shard_starts, queries, keys, values, ffn_weight)
        parts = [mine, shift(theirs, TALL, 1), shift(theirs, TALL, -1), shift(mine, TALL, 2)]
        q, kv, pair = align(shard_starts, own, up, down, parts)

    with jax.named_scope("weight_rows"):
        weight = lax.all_gather(pair, "z", axis=0, tiled=True)

    with jax.named_scope("keys_and_values"):
        far, near = z_blocks(kv)
        far1, near1 = (hop(a, (0, 1), (1, 2), (2, 3)) for a in (far, near))
        outer, inner = far[: HERE * TOK], far[HERE * TOK :]
        inner2 = hop(hop(inner, (1, 0), (0, 3)), (3, 2), (0, 3))
        outer2 = hop(hop(outer, (1, 0), (0, 3), below=HERE), (3, 2), (0, 3), below=HERE)
        state = attention(0, doc_lengths, q, [far, near], ())
        near1, far1, *state = lax.optimization_barrier((near1, far1, *state))
        near2 = hop(near1, (1, 2), (2, 3), below=FAR)

    with jax.named_scope("attention"):
        state = attention(1, doc_lengths, q, [far1, near1], state)
        (attended,) = attention(2, doc_lengths, q, [outer2, inner2, near2], state)

    gain = norm_gain.reshape(1, FEATURES)
    half = weight.shape[1]
    with jax.named_scope("features"):
        theirs = [shift_both(attended, 1, d) for d in (0, 1, -1, 2)]
        own = [attended] + [shift(attended, "x", d) for d in (1, -1, 2)]
        theirs, own = jnp.concatenate(theirs, axis=0), jnp.concatenate(own, axis=0)
        their_rows, their_inv = prepare(gain, theirs, shift(theirs, "c", 1))
        other = shift(own, "c", 1)

    with jax.named_scope("gate"):
        away = gate(their_rows, their_inv, weight, 0, SENT_FIRST)
        back = [shift(away, "yb", 1)]
        their_inv, away = lax.optimization_barrier((their_inv, away))
        rest = gate(their_rows, their_inv, weight, SENT_FIRST, half - SENT_FIRST)
        back.append(shift(rest, "yb", 1))
        gain, rest = lax.optimization_barrier((gain, rest))
        home = gate(*prepare(gain, own, other), weight, 0, half)
        return join(home, *back)


def solution(mesh):
    fine = Mesh(mesh.devices.reshape(NY // 2, 2, NZ, NX, NC), ("yp", "yb", "z", "x", "c"))
    return jax.shard_map(
        on_device,
        mesh=fine,
        in_specs=(P(ROWS, COLUMNS), P(ROWS, COLUMNS), P(ROWS, COLUMNS), P(), P(), P(), P(ROWS, COLUMNS)),
        out_specs=P(ROWS, COLUMNS),
        check_vma=False,
    )
```

```python
import functools

import jax
import jax.numpy as jnp
from jax import lax
from jax.experimental import pallas as pl
from jax.experimental.pallas import tpu as pltpu
from jax.sharding import Mesh, PartitionSpec as P

HD = 128
TOK = 256
CAP = 384
QUARTER = TOK // 4
FEATURES = 4096
TOKENS = 8192
NY, NZ, NX, NC = 4, 8, 4, 2
HEADS_HERE = 4
HERE = 2
FAR = 5
SENT_FIRST = 512
PARTS = 4
NORM_EPS = 1e-05
MASKED = -1e30
LOG2E = 1.4426950408889634
EXP2_SCALE = HD ** (-0.5) * LOG2E
VMEM = pl.BlockSpec(memory_space=pltpu.VMEM)
HBM = pl.BlockSpec(memory_space=pltpu.HBM)
SMEM = pl.BlockSpec(memory_space=pltpu.SMEM)
ROWS, COLUMNS, TALL = ("yp", "yb", "z"), ("x", "c"), ("yp", "yb")


def shift(block, axis, distance):
    count = lax.axis_size(axis)
    return lax.ppermute(block, axis, [(i, (i + distance) % count) for i in range(count)])


def here():
    y = lax.axis_index("yp") * 2 + lax.axis_index("yb")
    return y, lax.axis_index("z"), lax.axis_index("x"), lax.axis_index("c")


def hop(block, *route, below=NZ):
    return lax.ppermute(block, ROWS, [(a * NZ + z, b * NZ + z) for a, b in route for z in range(below)])


def shift_both(block, across, distance):
    pairs = [(b, i) for b in range(2) for i in range(NX)]
    to = lambda b, i: (b ^ across) * NX + (i + distance) % NX
    return lax.ppermute(block, ("yb", "x"), [(b * NX + i, to(b, i)) for b, i in pairs])


def z_blocks(block):
    up1, down1 = shift(block, "z", 1), shift(block, "z", -1)
    up2, down2 = shift(up1, "z", 1), shift(down1, "z", -1)
    far = jnp.concatenate([up2, up1, block, down1, down2], axis=0)
    up2, down2, far = lax.optimization_barrier((up2, down2, far))
    return far, jnp.concatenate([shift(down2, "z", -1), shift(up2, "z", 2), shift(up2, "z", 1)], axis=0)


def bf16(*shape):
    return jax.ShapeDtypeStruct(shape, jnp.bfloat16)


def f32(*shape):
    return jax.ShapeDtypeStruct(shape, jnp.float32)


def limit(mib):
    return pltpu.CompilerParams(vmem_limit_bytes=mib << 20)


def extent(starts):
    y, z, _, _ = here()
    mine = y * NZ + z
    after = jnp.where(mine == NY * NZ - 1, TOKENS, starts[jnp.minimum(mine + 1, NY * NZ - 1)])
    return starts[mine] - mine * TOK, after - mine * TOK


def open_kernel(starts, q, k, v, weight, own, up, down, theirs, mine, sems):
    first, _ = extent(starts)
    half, odd = weight.shape[1] // 2, lax.rem(here()[0], 2)
    column = lambda side: weight.at[:, pl.ds(pl.multiple_of(side * half, HD), half)]
    at, pairs = 0, []
    for ref in (q, k, v):
        pairs.append((ref, own.at[:, pl.ds(at, ref.shape[1])]))
        at += ref.shape[1]
    pairs += [(column(1 - odd), theirs), (column(odd), mine)]
    copies = [pltpu.make_async_copy(a, b, sems.at[i]) for i, (a, b) in enumerate(pairs)]
    for copy in copies:
        copy.start()
    for copy in copies:
        copy.wait()
    row = lax.broadcasted_iota(jnp.int32, (QUARTER, CAP), 0)
    slot = lax.broadcasted_iota(jnp.int32, (QUARTER, CAP), 1)
    picked = (slot == row + TOK - first).astype(jnp.bfloat16)
    up[...] = jnp.dot(picked, own[...], preferred_element_type=jnp.float32).astype(jnp.bfloat16)
    down[...] = own[:QUARTER]


def align_kernel(starts, rows, low, high, own_part, below, above, far_part, q_out, kv_out, pair, sems):
    depth = own_part.shape[0]
    copies = [
        pltpu.make_async_copy(part, pair.at[pl.ds(i * depth, depth)], sems.at[i])
        for i, part in enumerate((own_part, below, above, far_part))
    ]
    for copy in copies:
        copy.start()
    first, end = extent(starts)
    row = lax.broadcasted_iota(jnp.int32, (TOK, 1), 0)
    slot = lax.broadcasted_iota(jnp.int32, (TOK, CAP), 1)
    near = lax.broadcasted_iota(jnp.int32, (TOK, QUARTER), 1)
    own = ((slot == row - first) & (row >= first) & (row < end)).astype(jnp.bfloat16)
    from_low = ((near == row) & (row < first)).astype(jnp.bfloat16)
    from_high = ((near == row - end) & (row >= end)).astype(jnp.bfloat16)
    total = jnp.dot(own, rows[...], preferred_element_type=jnp.float32)
    total += jnp.dot(from_low, low[...], preferred_element_type=jnp.float32)
    total += jnp.dot(from_high, high[...], preferred_element_type=jnp.float32)
    wide = q_out.shape[1]
    q_out[...] = total[:, :wide].astype(jnp.bfloat16)
    kv_out[...] = total[:, wide:].astype(jnp.bfloat16)
    for copy in copies:
        copy.wait()


def in_hbm(array):
    return pltpu.with_memory_space_constraint(array, pltpu.HBM)


def opening(starts, q, k, v, weight):
    wide = q.shape[1] + k.shape[1] + v.shape[1]
    rows, half = weight.shape[0], weight.shape[1] // 2
    return pl.pallas_call(
        open_kernel,
        out_shape=(bf16(CAP, wide), *(bf16(QUARTER, wide),) * 2, *(bf16(rows, half),) * 2),
        in_specs=[SMEM] + [HBM] * 4,
        out_specs=(VMEM,) * 5,
        scratch_shapes=[pltpu.SemaphoreType.DMA((5,))],
        compiler_params=limit(16),
    )(*(in_hbm(a) for a in (starts, q, k, v, weight)))


def align(starts, own, up, down, parts):
    count = NY * NZ
    low = lax.ppermute(up, ROWS, [(i, (i + 1) % count) for i in range(count)])
    high = lax.ppermute(down, ROWS, [(i, (i - 1) % count) for i in range(count)])
    depth, columns = parts[0].shape
    return pl.pallas_call(
        align_kernel,
        out_shape=(bf16(TOK, HEADS_HERE * HD), bf16(TOK, 2 * HD), bf16(NY * depth, columns)),
        in_specs=[SMEM] + [VMEM] * 7,
        out_specs=(VMEM, VMEM, HBM),
        scratch_shapes=[pltpu.SemaphoreType.DMA((4,))],
        compiler_params=limit(16),
    )(in_hbm(starts), own, low, high, *parts)


def attention_kernel(back, parts, place, lengths, q_ref, *refs):
    blocks, refs = refs[:parts], refs[parts:]
    if back:
        old_stats, old_sums, *refs = refs
    if back == 2:
        out_ref, stats, sums = refs
    else:
        stats, sums = refs
    y, z = place() if callable(place) else place
    ends, total = [], 0
    for i in range(4):
        total += lengths[i]
        ends.append(total)
    mine = y * NZ + z
    query = mine * TOK + lax.broadcasted_iota(jnp.int32, (1, TOK), 1)

    def start_of(token):
        start = token * 0
        for end in ends:
            start = jnp.maximum(start, jnp.where(end <= token, end, 0))
        return start

    starts = start_of(query)
    lowest = start_of(mine * TOK) // TOK
    clear = (start_of(mine * TOK + TOK - 1) + TOK - 1) // TOK

    def step(ref, row, block, masked, opening):
        key, value = ref[pl.ds(row, TOK), :HD], ref[pl.ds(row, TOK), HD:]
        heads = range(HEADS_HERE)
        scores = [
            lax.dot_general(
                key, q_ref[:, h * HD : (h + 1) * HD], (((1,), (1,)), ((), ())), preferred_element_type=jnp.float32
            )
            for h in heads
        ]
        if masked:
            ids = block * TOK + lax.broadcasted_iota(jnp.int32, (TOK, 1), 0)
            allowed = (ids >= starts) & (ids <= query)
            scores = [jnp.where(allowed, s, MASKED) for s in scores]
        tops = [jnp.max(s, axis=0, keepdims=True) * EXP2_SCALE for s in scores]
        if not opening:
            was = [stats[h : h + 1] for h in heads]
            tops = [jnp.maximum(a, b) for a, b in zip(tops, was)]
            fading = [jnp.exp2(a - b) for a, b in zip(was, tops)]
        weights = [jnp.exp2(s * EXP2_SCALE - t) for s, t in zip(scores, tops)]
        mass = [jnp.sum(w, axis=0, keepdims=True) for w in weights]
        added = [
            lax.dot_general(
                value, w.astype(jnp.bfloat16), (((0,), (0,)), ((), ())), preferred_element_type=jnp.float32
            )
            for w in weights
        ]
        if not opening:
            mass = [m + stats[4 + h : 5 + h] * f for h, m, f in zip(heads, mass, fading)]
            added = [a + sums[h] * f for h, a, f in zip(heads, added, fading)]
        for h in heads:
            stats[h : h + 1] = tops[h]
            stats[4 + h : 5 + h] = mass[h]
            sums[h] = added[h]

    if back:
        stats[...] = old_stats[...]
        sums[...] = old_sums[...]
    else:
        step(blocks[0], HERE * TOK, mine, True, True)
    before = 0
    for ref in blocks:

        def body(i, _, ref=ref, before=before):
            block = (y - back) * NZ + lax.rem(z + before + i - HERE + NZ, NZ)
            needed = (block >= lowest) & (block < mine)
            row = pl.multiple_of(i * TOK, TOK)

            @pl.when(needed & (block < clear))
            def _():
                step(ref, row, block, True, False)

            @pl.when(needed & (block >= clear))
            def _():
                step(ref, row, block, False, False)

            return 0

        lax.fori_loop(0, ref.shape[0] // TOK, body, 0)
        before += ref.shape[0] // TOK
    if back == 2:
        for h in range(HEADS_HERE):
            out_ref[:, h * HD : (h + 1) * HD] = (sums[h] / stats[4 + h : 5 + h]).T.astype(jnp.bfloat16)


def attention(back, lengths, q, blocks, state, place=lambda: here()[:2]):
    shapes = [f32(2 * HEADS_HERE, TOK), f32(HEADS_HERE, HD, TOK)]
    kwargs = {}
    if back == 2:
        kwargs["scratch_shapes"] = [pltpu.VMEM(s.shape, s.dtype) for s in shapes]
        shapes = [bf16(TOK, HEADS_HERE * HD)]
    work = 8 * HEADS_HERE * TOK * TOK
    return pl.pallas_call(
        functools.partial(attention_kernel, back, len(blocks), place),
        out_shape=tuple(shapes),
        in_specs=[SMEM] + [VMEM] * (1 + len(blocks) + len(state)),
        out_specs=(VMEM,) * len(shapes),
        compiler_params=limit(32),
        cost_estimate=pl.CostEstimate(flops=4 * work * HD, bytes_accessed=4 << 20, transcendentals=work),
        **kwargs,
    )(lengths, q, *blocks, *state)


def prepare_kernel(gain, mine, other, rows, inv):
    y, _, x, c = here()
    squares = jnp.zeros((TOK, HD), jnp.float32)
    for side, pieces in enumerate((mine, other)):
        for i in range(NX):
            tp = lax.rem(x + (0, 3, 1, 2)[i], NX) * NC + (c if side == 0 else 1 - c)
            for j in range(HEADS_HERE):
                head = tp * HEADS_HERE + j
                part = pieces[i * TOK : (i + 1) * TOK, j * HD : (j + 1) * HD].astype(jnp.float32)
                squares += part * part
                scaled = (part * gain[:, pl.ds(pl.multiple_of(head * HD, HD), HD)]).astype(jnp.bfloat16)
                away = lax.rem(head // NZ - y + NY, NY)
                slot = jnp.where(away == 0, 0, jnp.where(away == 3, 1, away + 1))
                place = lax.rem(head, NZ) * NY + slot
                rows[:, pl.ds(pl.multiple_of(place * HD, HD), HD)] = scaled
    mean = jnp.sum(squares, axis=1, keepdims=True) / FEATURES
    inv[...] = jnp.broadcast_to(lax.rsqrt(mean + NORM_EPS), (TOK, HD))


def prepare(gain, mine, other):
    return pl.pallas_call(
        prepare_kernel,
        out_shape=(bf16(TOK, FEATURES), f32(TOK, HD)),
        in_specs=[VMEM] * 3,
        out_specs=(VMEM,) * 2,
        compiler_params=limit(16),
    )(gain, mine, other)


def silu(value):
    return (value / (1.0 + jnp.exp(-value))).astype(jnp.bfloat16)


def first_gate_kernel(rows, inv, weight, out, held, total, sems):
    depth = FEATURES // PARTS
    sent = out.shape[1]
    parts = [pl.ds(i * depth, depth) for i in range(PARTS)]
    spots = [(p, c) for c in (pl.ds(0, sent), pl.ds(sent, held.shape[1] - sent)) for p in parts]
    copies = [pltpu.make_async_copy(weight.at[s], held.at[s], sems.at[i]) for i, s in enumerate(spots)]
    for copy in copies:
        copy.start()
    for i in range(PARTS):
        copies[i].wait()
        term = jnp.dot(
            rows[:, i * depth : (i + 1) * depth],
            held[i * depth : (i + 1) * depth, :sent],
            preferred_element_type=jnp.float32,
        )
        if i == 0:
            total[...] = term
        elif i < PARTS - 1:
            total[...] += term
        else:
            out[...] = silu((total[...] + term) * inv[:, :1])
    for copy in copies[PARTS:]:
        copy.wait()


def first_gate(rows, inv, weight):
    return pl.pallas_call(
        first_gate_kernel,
        out_shape=(bf16(TOK, SENT_FIRST), bf16(*weight.shape)),
        in_specs=[VMEM] * 2 + [HBM],
        out_specs=(VMEM,) * 2,
        scratch_shapes=[pltpu.VMEM((TOK, SENT_FIRST), jnp.float32), pltpu.SemaphoreType.DMA((2 * PARTS,))],
        compiler_params=limit(20),
    )(rows, inv, in_hbm(weight))


def gate_kernel(first, rows, inv, weight, out):
    for at in range(0, out.shape[1], 2 * HD):
        end = min(at + 2 * HD, out.shape[1])
        value = jnp.dot(rows[...], weight[:, first + at : first + end], preferred_element_type=jnp.float32)
        out[:, at:end] = silu(value * inv[:, :1])


def gate(rows, inv, weight, first, columns):
    return pl.pallas_call(
        functools.partial(gate_kernel, first),
        out_shape=bf16(TOK, columns),
        in_specs=[VMEM] * 3,
        out_specs=VMEM,
        compiler_params=limit(20),
        cost_estimate=pl.CostEstimate(
            flops=2 * TOK * FEATURES * columns, bytes_accessed=2 * FEATURES * columns, transcendentals=TOK * columns
        ),
    )(rows, inv, weight)


def join_kernel(*refs):
    *parts, out = refs
    half, odd = out.shape[1] // 2, lax.rem(here()[0], 2)
    at = 0
    for ref in parts:
        side = odd if at < half else 1 - odd
        place = side * half + at % half
        out[:, pl.ds(pl.multiple_of(place, HD), ref.shape[1])] = ref[...]
        at += ref.shape[1]


def join(*parts):
    return pl.pallas_call(
        join_kernel,
        out_shape=bf16(TOK, sum(part.shape[1] for part in parts)),
        in_specs=[VMEM] * len(parts),
        out_specs=VMEM,
        compiler_params=limit(8),
    )(*parts)


def on_device(queries, keys, values, doc_lengths, shard_starts, norm_gain, ffn_weight):
    with jax.named_scope("rows_to_owners"):
        own, up, down, theirs, mine = opening(shard_starts, queries, keys, values, ffn_weight)
        far_part = shift(mine, TALL, 2)
        parts = [mine, shift(theirs, TALL, 1), shift(theirs, TALL, -1), far_part]
        q, kv, pair = align(shard_starts, own, up, down, parts)

    with jax.named_scope("weight_rows"):
        weight = lax.all_gather(pair, "z", axis=0, tiled=True)

    with jax.named_scope("keys_and_values"):
        far, near = z_blocks(kv)
        far1, near1 = (hop(a, (0, 1), (1, 2), (2, 3)) for a in (far, near))
        outer, inner = far[: HERE * TOK], far[HERE * TOK :]
        inner2 = hop(hop(inner, (1, 0), (0, 3)), (3, 2), (0, 3))
        outer2 = hop(hop(outer, (1, 0), (0, 3), below=HERE), (3, 2), (0, 3), below=HERE)
        state = attention(0, doc_lengths, q, [far, near], ())
        near1, far1, *state = lax.optimization_barrier((near1, far1, *state))
        near2 = hop(near1, (1, 2), (2, 3), below=FAR)

    with jax.named_scope("attention"):
        state = attention(1, doc_lengths, q, [far1, near1], state)
        (attended,) = attention(2, doc_lengths, q, [outer2, inner2, near2], state)

    gain = norm_gain.reshape(1, FEATURES)
    half = weight.shape[1]
    with jax.named_scope("features"):
        theirs = [shift_both(attended, 1, d) for d in (0, 1, -1, 2)]
        own = [attended] + [shift(attended, "x", d) for d in (1, -1, 2)]
        theirs, own = jnp.concatenate(theirs, axis=0), jnp.concatenate(own, axis=0)
        their_rows, their_inv = prepare(gain, theirs, shift(theirs, "c", 1))
        other = shift(own, "c", 1)

    with jax.named_scope("gate"):
        away, held = first_gate(their_rows, their_inv, weight)
        back = [shift(away, "yb", 1)]
        their_inv, away = lax.optimization_barrier((their_inv, away))
        rest = gate(their_rows, their_inv, held, SENT_FIRST, half - SENT_FIRST)
        back.append(shift(rest, "yb", 1))
        gain, rest = lax.optimization_barrier((gain, rest))
        home = gate(*prepare(gain, own, other), held, 0, half)
        return join(home, *back)


def solution(mesh):
    fine = Mesh(mesh.devices.reshape(NY // 2, 2, NZ, NX, NC), ("yp", "yb", "z", "x", "c"))
    return jax.shard_map(
        on_device,
        mesh=fine,
        in_specs=(P(ROWS, COLUMNS), P(ROWS, COLUMNS), P(ROWS, COLUMNS), P(), P(), P(), P(ROWS, COLUMNS)),
        out_specs=P(ROWS, COLUMNS),
        check_vma=False,
    )
```

```python
import functools

import jax
import jax.numpy as jnp
from jax import lax
from jax.experimental import pallas as pl
from jax.experimental.pallas import tpu as pltpu
from jax.sharding import Mesh, PartitionSpec as P

HD = 128
TOK = 256
CAP = 384
QUARTER = TOK // 4
FEATURES = 4096
TOKENS = 8192
NY, NZ, NX, NC = 4, 8, 4, 2
HEADS_HERE = 4
HERE = 2
FAR = 5
SENT_FIRST = 640
PARTS = 4
NORM_EPS = 1e-05
MASKED = -1e30
LOG2E = 1.4426950408889634
EXP2_SCALE = HD ** (-0.5) * LOG2E
VMEM = pl.BlockSpec(memory_space=pltpu.VMEM)
HBM = pl.BlockSpec(memory_space=pltpu.HBM)
SMEM = pl.BlockSpec(memory_space=pltpu.SMEM)
ROWS, COLUMNS, TALL = ("yp", "yb", "z"), ("x", "c"), ("yp", "yb")


def shift(block, axis, distance):
    count = lax.axis_size(axis)
    return lax.ppermute(block, axis, [(i, (i + distance) % count) for i in range(count)])


def here():
    y = lax.axis_index("yp") * 2 + lax.axis_index("yb")
    return y, lax.axis_index("z"), lax.axis_index("x"), lax.axis_index("c")


def hop(block, *route, below=NZ):
    return lax.ppermute(block, ROWS, [(a * NZ + z, b * NZ + z) for a, b in route for z in range(below)])


def shift_both(block, across, distance):
    pairs = [(b, i) for b in range(2) for i in range(NX)]
    to = lambda b, i: (b ^ across) * NX + (i + distance) % NX
    return lax.ppermute(block, ("yb", "x"), [(b * NX + i, to(b, i)) for b, i in pairs])


def z_blocks(block):
    up1, down1 = shift(block, "z", 1), shift(block, "z", -1)
    up2, down2 = shift(up1, "z", 1), shift(down1, "z", -1)
    far = jnp.concatenate([up2, up1, block, down1, down2], axis=0)
    up2, down2, far = lax.optimization_barrier((up2, down2, far))
    return far, jnp.concatenate([shift(down2, "z", -1), shift(up2, "z", 2), shift(up2, "z", 1)], axis=0)


def bf16(*shape):
    return jax.ShapeDtypeStruct(shape, jnp.bfloat16)


def f32(*shape):
    return jax.ShapeDtypeStruct(shape, jnp.float32)


def limit(mib):
    return pltpu.CompilerParams(vmem_limit_bytes=mib << 20)


def extent(starts):
    y, z, _, _ = here()
    mine = y * NZ + z
    after = jnp.where(mine == NY * NZ - 1, TOKENS, starts[jnp.minimum(mine + 1, NY * NZ - 1)])
    return starts[mine] - mine * TOK, after - mine * TOK


def open_kernel(starts, q, k, v, weight, own, up, down, theirs, mine, sems):
    first, _ = extent(starts)
    half, odd = weight.shape[1] // 2, lax.rem(here()[0], 2)
    column = lambda side: weight.at[:, pl.ds(pl.multiple_of(side * half, HD), half)]
    at, pairs = 0, []
    for ref in (q, k, v):
        pairs.append((ref, own.at[:, pl.ds(at, ref.shape[1])]))
        at += ref.shape[1]
    pairs += [(column(1 - odd), theirs), (column(odd), mine)]
    copies = [pltpu.make_async_copy(a, b, sems.at[i]) for i, (a, b) in enumerate(pairs)]
    for copy in copies:
        copy.start()
    for copy in copies:
        copy.wait()
    row = lax.broadcasted_iota(jnp.int32, (QUARTER, CAP), 0)
    slot = lax.broadcasted_iota(jnp.int32, (QUARTER, CAP), 1)
    picked = (slot == row + TOK - first).astype(jnp.bfloat16)
    up[...] = jnp.dot(picked, own[...], preferred_element_type=jnp.float32).astype(jnp.bfloat16)
    down[...] = own[:QUARTER]


def align_kernel(starts, rows, low, high, own_part, below, above, far_part, q_out, kv_out, pair, sems):
    depth = own_part.shape[0]
    copies = [
        pltpu.make_async_copy(part, pair.at[pl.ds(i * depth, depth)], sems.at[i])
        for i, part in enumerate((own_part, below, above, far_part))
    ]
    for copy in copies:
        copy.start()
    first, end = extent(starts)
    row = lax.broadcasted_iota(jnp.int32, (TOK, 1), 0)
    slot = lax.broadcasted_iota(jnp.int32, (TOK, CAP), 1)
    near = lax.broadcasted_iota(jnp.int32, (TOK, QUARTER), 1)
    own = ((slot == row - first) & (row >= first) & (row < end)).astype(jnp.bfloat16)
    from_low = ((near == row) & (row < first)).astype(jnp.bfloat16)
    from_high = ((near == row - end) & (row >= end)).astype(jnp.bfloat16)
    total = jnp.dot(own, rows[...], preferred_element_type=jnp.float32)
    total += jnp.dot(from_low, low[...], preferred_element_type=jnp.float32)
    total += jnp.dot(from_high, high[...], preferred_element_type=jnp.float32)
    wide = q_out.shape[1]
    q_out[...] = total[:, :wide].astype(jnp.bfloat16)
    kv_out[...] = total[:, wide:].astype(jnp.bfloat16)
    for copy in copies:
        copy.wait()


def in_hbm(array):
    return pltpu.with_memory_space_constraint(array, pltpu.HBM)


def opening(starts, q, k, v, weight):
    wide = q.shape[1] + k.shape[1] + v.shape[1]
    rows, half = weight.shape[0], weight.shape[1] // 2
    return pl.pallas_call(
        open_kernel,
        out_shape=(bf16(CAP, wide), *(bf16(QUARTER, wide),) * 2, *(bf16(rows, half),) * 2),
        in_specs=[SMEM] + [HBM] * 4,
        out_specs=(VMEM,) * 5,
        scratch_shapes=[pltpu.SemaphoreType.DMA((5,))],
        compiler_params=limit(16),
    )(*(in_hbm(a) for a in (starts, q, k, v, weight)))


def align(starts, own, up, down, parts):
    count = NY * NZ
    low = lax.ppermute(up, ROWS, [(i, (i + 1) % count) for i in range(count)])
    high = lax.ppermute(down, ROWS, [(i, (i - 1) % count) for i in range(count)])
    depth, columns = parts[0].shape
    return pl.pallas_call(
        align_kernel,
        out_shape=(bf16(TOK, HEADS_HERE * HD), bf16(TOK, 2 * HD), bf16(NY * depth, columns)),
        in_specs=[SMEM] + [VMEM] * 7,
        out_specs=(VMEM, VMEM, HBM),
        scratch_shapes=[pltpu.SemaphoreType.DMA((4,))],
        compiler_params=limit(16),
    )(in_hbm(starts), own, low, high, *parts)


def attention_kernel(back, parts, place, lengths, q_ref, *refs):
    blocks, refs = refs[:parts], refs[parts:]
    if back:
        old_stats, old_sums, *refs = refs
    if back == 2:
        out_ref, stats, sums = refs
    else:
        stats, sums = refs
    y, z = place() if callable(place) else place
    ends, total = [], 0
    for i in range(4):
        total += lengths[i]
        ends.append(total)
    mine = y * NZ + z
    query = mine * TOK + lax.broadcasted_iota(jnp.int32, (1, TOK), 1)

    def start_of(token):
        start = token * 0
        for end in ends:
            start = jnp.maximum(start, jnp.where(end <= token, end, 0))
        return start

    starts = start_of(query)
    lowest = start_of(mine * TOK) // TOK
    clear = (start_of(mine * TOK + TOK - 1) + TOK - 1) // TOK

    def step(ref, row, block, masked, opening):
        key, value = ref[pl.ds(row, TOK), :HD], ref[pl.ds(row, TOK), HD:]
        heads = range(HEADS_HERE)
        scores = [
            lax.dot_general(
                key, q_ref[:, h * HD : (h + 1) * HD], (((1,), (1,)), ((), ())), preferred_element_type=jnp.float32
            )
            for h in heads
        ]
        if masked:
            ids = block * TOK + lax.broadcasted_iota(jnp.int32, (TOK, 1), 0)
            allowed = (ids >= starts) & (ids <= query)
            scores = [jnp.where(allowed, s, MASKED) for s in scores]
        tops = [jnp.max(s, axis=0, keepdims=True) * EXP2_SCALE for s in scores]
        if not opening:
            was = [stats[h : h + 1] for h in heads]
            tops = [jnp.maximum(a, b) for a, b in zip(tops, was)]
            fading = [jnp.exp2(a - b) for a, b in zip(was, tops)]
        weights = [jnp.exp2(s * EXP2_SCALE - t) for s, t in zip(scores, tops)]
        mass = [jnp.sum(w, axis=0, keepdims=True) for w in weights]
        added = [
            lax.dot_general(
                value, w.astype(jnp.bfloat16), (((0,), (0,)), ((), ())), preferred_element_type=jnp.float32
            )
            for w in weights
        ]
        if not opening:
            mass = [m + stats[4 + h : 5 + h] * f for h, m, f in zip(heads, mass, fading)]
            added = [a + sums[h] * f for h, a, f in zip(heads, added, fading)]
        for h in heads:
            stats[h : h + 1] = tops[h]
            stats[4 + h : 5 + h] = mass[h]
            sums[h] = added[h]

    if back:
        stats[...] = old_stats[...]
        sums[...] = old_sums[...]
    else:
        step(blocks[0], HERE * TOK, mine, True, True)
    before = 0
    for ref in blocks:

        def body(i, _, ref=ref, before=before):
            block = (y - back) * NZ + lax.rem(z + before + i - HERE + NZ, NZ)
            needed = (block >= lowest) & (block < mine)
            row = pl.multiple_of(i * TOK, TOK)

            @pl.when(needed & (block < clear))
            def _():
                step(ref, row, block, True, False)

            @pl.when(needed & (block >= clear))
            def _():
                step(ref, row, block, False, False)

            return 0

        lax.fori_loop(0, ref.shape[0] // TOK, body, 0)
        before += ref.shape[0] // TOK
    if back == 2:
        for h in range(HEADS_HERE):
            out_ref[:, h * HD : (h + 1) * HD] = (sums[h] / stats[4 + h : 5 + h]).T.astype(jnp.bfloat16)


def attention(back, lengths, q, blocks, state, place=lambda: here()[:2]):
    shapes = [f32(2 * HEADS_HERE, TOK), f32(HEADS_HERE, HD, TOK)]
    kwargs = {}
    if back == 2:
        kwargs["scratch_shapes"] = [pltpu.VMEM(s.shape, s.dtype) for s in shapes]
        shapes = [bf16(TOK, HEADS_HERE * HD)]
    work = 8 * HEADS_HERE * TOK * TOK
    return pl.pallas_call(
        functools.partial(attention_kernel, back, len(blocks), place),
        out_shape=tuple(shapes),
        in_specs=[SMEM] + [VMEM] * (1 + len(blocks) + len(state)),
        out_specs=(VMEM,) * len(shapes),
        compiler_params=limit(32),
        cost_estimate=pl.CostEstimate(flops=4 * work * HD, bytes_accessed=4 << 20, transcendentals=work),
        **kwargs,
    )(lengths, q, *blocks, *state)


def prepare_kernel(gain, mine, other, rows, inv):
    y, _, x, c = here()
    squares = jnp.zeros((TOK, HD), jnp.float32)
    for side, pieces in enumerate((mine, other)):
        for i in range(NX):
            tp = lax.rem(x + (0, 3, 1, 2)[i], NX) * NC + (c if side == 0 else 1 - c)
            for j in range(HEADS_HERE):
                head = tp * HEADS_HERE + j
                part = pieces[i * TOK : (i + 1) * TOK, j * HD : (j + 1) * HD].astype(jnp.float32)
                squares += part * part
                scaled = (part * gain[:, pl.ds(pl.multiple_of(head * HD, HD), HD)]).astype(jnp.bfloat16)
                away = lax.rem(head // NZ - y + NY, NY)
                slot = jnp.where(away == 0, 0, jnp.where(away == 3, 1, away + 1))
                place = lax.rem(head, NZ) * NY + slot
                rows[:, pl.ds(pl.multiple_of(place * HD, HD), HD)] = scaled
    mean = jnp.sum(squares, axis=1, keepdims=True) / FEATURES
    inv[...] = jnp.broadcast_to(lax.rsqrt(mean + NORM_EPS), (TOK, HD))


def prepare(gain, mine, other):
    return pl.pallas_call(
        prepare_kernel,
        out_shape=(bf16(TOK, FEATURES), f32(TOK, HD)),
        in_specs=[VMEM] * 3,
        out_specs=(VMEM,) * 2,
        compiler_params=limit(16),
    )(gain, mine, other)


def silu(value):
    return (value / (1.0 + jnp.exp(-value))).astype(jnp.bfloat16)


def first_gate_kernel(rows, inv, weight, out, held, total, sems):
    depth = FEATURES // PARTS
    sent = out.shape[1]
    parts = [pl.ds(i * depth, depth) for i in range(PARTS)]
    spots = [(p, c) for c in (pl.ds(0, sent), pl.ds(sent, held.shape[1] - sent)) for p in parts]
    copies = [pltpu.make_async_copy(weight.at[s], held.at[s], sems.at[i]) for i, s in enumerate(spots)]
    for copy in copies:
        copy.start()
    for i in range(PARTS):
        copies[i].wait()
        term = jnp.dot(
            rows[:, i * depth : (i + 1) * depth],
            held[i * depth : (i + 1) * depth, :sent],
            preferred_element_type=jnp.float32,
        )
        if i == 0:
            total[...] = term
        elif i < PARTS - 1:
            total[...] += term
        else:
            out[...] = silu((total[...] + term) * inv[:, :1])
    for copy in copies[PARTS:]:
        copy.wait()


def first_gate(rows, inv, weight):
    return pl.pallas_call(
        first_gate_kernel,
        out_shape=(bf16(TOK, SENT_FIRST), bf16(*weight.shape)),
        in_specs=[VMEM] * 2 + [HBM],
        out_specs=(VMEM,) * 2,
        scratch_shapes=[pltpu.VMEM((TOK, SENT_FIRST), jnp.float32), pltpu.SemaphoreType.DMA((2 * PARTS,))],
        compiler_params=limit(20),
    )(rows, inv, in_hbm(weight))


def gate_kernel(first, rows, inv, weight, out):
    for at in range(0, out.shape[1], 2 * HD):
        end = min(at + 2 * HD, out.shape[1])
        value = jnp.dot(rows[...], weight[:, first + at : first + end], preferred_element_type=jnp.float32)
        out[:, at:end] = silu(value * inv[:, :1])


def gate(rows, inv, weight, first, columns):
    return pl.pallas_call(
        functools.partial(gate_kernel, first),
        out_shape=bf16(TOK, columns),
        in_specs=[VMEM] * 3,
        out_specs=VMEM,
        compiler_params=limit(20),
        cost_estimate=pl.CostEstimate(
            flops=2 * TOK * FEATURES * columns, bytes_accessed=2 * FEATURES * columns, transcendentals=TOK * columns
        ),
    )(rows, inv, weight)


def home_kernel(rows, inv, weight, out):
    half = weight.shape[1]
    side = lax.rem(here()[0], 2) * half
    for at in range(0, half, 2 * HD):
        end = min(at + 2 * HD, half)
        value = jnp.dot(rows[...], weight[:, at:end], preferred_element_type=jnp.float32)
        out[:, pl.ds(pl.multiple_of(side + at, HD), end - at)] = silu(value * inv[:, :1])


def home_gate(rows, inv, weight):
    columns = weight.shape[1]
    return pl.pallas_call(
        home_kernel,
        out_shape=bf16(TOK, 2 * columns),
        in_specs=[VMEM] * 3,
        out_specs=VMEM,
        compiler_params=limit(20),
        cost_estimate=pl.CostEstimate(
            flops=2 * TOK * FEATURES * columns, bytes_accessed=2 * FEATURES * columns, transcendentals=TOK * columns
        ),
    )(rows, inv, weight)


def join_kernel(first, rest, _, out, sems):
    half = out.shape[1] // 2
    at = (1 - lax.rem(here()[0], 2)) * half
    copies = []
    for i, part in enumerate((first, rest)):
        place = out.at[:, pl.ds(pl.multiple_of(at, HD), part.shape[1])]
        copies.append(pltpu.make_async_copy(part, place, sems.at[i]))
        at += part.shape[1]
    for copy in copies:
        copy.start()
    for copy in copies:
        copy.wait()


def join(out, first, rest):
    return pl.pallas_call(
        join_kernel,
        out_shape=bf16(*out.shape),
        in_specs=[VMEM] * 2 + [HBM],
        out_specs=HBM,
        scratch_shapes=[pltpu.SemaphoreType.DMA((2,))],
        input_output_aliases={2: 0},
        compiler_params=limit(8),
    )(first, rest, out)


def on_device(queries, keys, values, doc_lengths, shard_starts, norm_gain, ffn_weight):
    with jax.named_scope("rows_to_owners"):
        own, up, down, theirs, mine = opening(shard_starts, queries, keys, values, ffn_weight)
        far_part = shift(mine, TALL, 2)
        parts = [mine, shift(theirs, TALL, 1), shift(theirs, TALL, -1), far_part]
        q, kv, pair = align(shard_starts, own, up, down, parts)

    with jax.named_scope("weight_rows"):
        weight = lax.all_gather(pair, "z", axis=0, tiled=True)

    with jax.named_scope("keys_and_values"):
        far, near = z_blocks(kv)
        far1, near1 = (hop(a, (0, 1), (1, 2), (2, 3)) for a in (far, near))
        outer, inner = far[: HERE * TOK], far[HERE * TOK :]
        inner2 = hop(hop(inner, (1, 0), (0, 3)), (3, 2), (0, 3))
        outer2 = hop(hop(outer, (1, 0), (0, 3), below=HERE), (3, 2), (0, 3), below=HERE)
        state = attention(0, doc_lengths, q, [far, near], ())
        near1, far1, *state = lax.optimization_barrier((near1, far1, *state))
        near2 = hop(near1, (1, 2), (2, 3), below=FAR)

    with jax.named_scope("attention"):
        state = attention(1, doc_lengths, q, [far1, near1], state)
        (attended,) = attention(2, doc_lengths, q, [outer2, inner2, near2], state)

    gain = norm_gain.reshape(1, FEATURES)
    half = weight.shape[1]
    with jax.named_scope("features"):
        theirs = [shift_both(attended, 1, d) for d in (0, 1, -1, 2)]
        own = [attended] + [shift(attended, "x", d) for d in (1, -1, 2)]
        theirs, own = jnp.concatenate(theirs, axis=0), jnp.concatenate(own, axis=0)
        their_rows, their_inv = prepare(gain, theirs, shift(theirs, "c", 1))
        other = shift(own, "c", 1)

    with jax.named_scope("gate"):
        away, held = first_gate(their_rows, their_inv, weight)
        back = [shift(away, "yb", 1)]
        their_inv, away = lax.optimization_barrier((their_inv, away))
        rest = gate(their_rows, their_inv, held, SENT_FIRST, half - SENT_FIRST)
        back.append(shift(rest, "yb", 1))
        gain, rest = lax.optimization_barrier((gain, rest))
        return join(home_gate(*prepare(gain, own, other), held), *back)


def solution(mesh):
    fine = Mesh(mesh.devices.reshape(NY // 2, 2, NZ, NX, NC), ("yp", "yb", "z", "x", "c"))
    return jax.shard_map(
        on_device,
        mesh=fine,
        in_specs=(P(ROWS, COLUMNS), P(ROWS, COLUMNS), P(ROWS, COLUMNS), P(), P(), P(), P(ROWS, COLUMNS)),
        out_specs=P(ROWS, COLUMNS),
        check_vma=False,
    )
```

```python
import functools

import jax
import jax.numpy as jnp
from jax import lax
from jax.experimental import pallas as pl
from jax.experimental.pallas import tpu as pltpu
from jax.sharding import Mesh, PartitionSpec as P

HD = 128
TOK = 256
CAP = 384
QUARTER = TOK // 4
FEATURES = 4096
TOKENS = 8192
NY, NZ, NX, NC = 4, 8, 4, 2
HEADS_HERE = 4
HERE = 2
FAR = 5
SENT_FIRST = 512
PARTS = 2
NORM_EPS = 1e-05
MASKED = -1e30
LOG2E = 1.4426950408889634
EXP2_SCALE = HD ** (-0.5) * LOG2E
VMEM = pl.BlockSpec(memory_space=pltpu.VMEM)
HBM = pl.BlockSpec(memory_space=pltpu.HBM)
SMEM = pl.BlockSpec(memory_space=pltpu.SMEM)
ROWS, COLUMNS, TALL = ("yp", "yb", "z"), ("x", "c"), ("yp", "yb")


def shift(block, axis, distance):
    count = lax.axis_size(axis)
    return lax.ppermute(block, axis, [(i, (i + distance) % count) for i in range(count)])


def here():
    y = lax.axis_index("yp") * 2 + lax.axis_index("yb")
    return y, lax.axis_index("z"), lax.axis_index("x"), lax.axis_index("c")


def hop(block, *route, below=NZ):
    return lax.ppermute(block, ROWS, [(a * NZ + z, b * NZ + z) for a, b in route for z in range(below)])


def shift_both(block, across, distance):
    pairs = [(b, i) for b in range(2) for i in range(NX)]
    to = lambda b, i: (b ^ across) * NX + (i + distance) % NX
    return lax.ppermute(block, ("yb", "x"), [(b * NX + i, to(b, i)) for b, i in pairs])


def z_blocks(block):
    up1, down1 = shift(block, "z", 1), shift(block, "z", -1)
    up2, down2 = shift(up1, "z", 1), shift(down1, "z", -1)
    far = jnp.concatenate([up2, up1, block, down1, down2], axis=0)
    up2, down2, far = lax.optimization_barrier((up2, down2, far))
    return far, jnp.concatenate([shift(down2, "z", -1), shift(up2, "z", 2), shift(up2, "z", 1)], axis=0)


def bf16(*shape):
    return jax.ShapeDtypeStruct(shape, jnp.bfloat16)


def f32(*shape):
    return jax.ShapeDtypeStruct(shape, jnp.float32)


def limit(mib):
    return pltpu.CompilerParams(vmem_limit_bytes=mib << 20)


def extent(starts):
    y, z, _, _ = here()
    mine = y * NZ + z
    after = jnp.where(mine == NY * NZ - 1, TOKENS, starts[jnp.minimum(mine + 1, NY * NZ - 1)])
    return starts[mine] - mine * TOK, after - mine * TOK


def open_kernel(starts, q, k, v, weight, own, up, down, theirs, mine, sems):
    first, _ = extent(starts)
    half, odd = weight.shape[1] // 2, lax.rem(here()[0], 2)
    column = lambda side: weight.at[:, pl.ds(pl.multiple_of(side * half, HD), half)]
    at, pairs = 0, []
    for ref in (q, k, v):
        pairs.append((ref, own.at[:, pl.ds(at, ref.shape[1])]))
        at += ref.shape[1]
    pairs += [(column(1 - odd), theirs), (column(odd), mine)]
    copies = [pltpu.make_async_copy(a, b, sems.at[i]) for i, (a, b) in enumerate(pairs)]
    for copy in copies:
        copy.start()
    for copy in copies:
        copy.wait()
    row = lax.broadcasted_iota(jnp.int32, (QUARTER, CAP), 0)
    slot = lax.broadcasted_iota(jnp.int32, (QUARTER, CAP), 1)
    picked = (slot == row + TOK - first).astype(jnp.bfloat16)
    up[...] = jnp.dot(picked, own[...], preferred_element_type=jnp.float32).astype(jnp.bfloat16)
    down[...] = own[:QUARTER]


def align_kernel(starts, rows, low, high, own_part, below, above, far_part, q_out, kv_out, pair, sems):
    depth = own_part.shape[0]
    copies = [
        pltpu.make_async_copy(part, pair.at[pl.ds(i * depth, depth)], sems.at[i])
        for i, part in enumerate((own_part, below, above, far_part))
    ]
    for copy in copies:
        copy.start()
    first, end = extent(starts)
    row = lax.broadcasted_iota(jnp.int32, (TOK, 1), 0)
    slot = lax.broadcasted_iota(jnp.int32, (TOK, CAP), 1)
    near = lax.broadcasted_iota(jnp.int32, (TOK, QUARTER), 1)
    own = ((slot == row - first) & (row >= first) & (row < end)).astype(jnp.bfloat16)
    from_low = ((near == row) & (row < first)).astype(jnp.bfloat16)
    from_high = ((near == row - end) & (row >= end)).astype(jnp.bfloat16)
    total = jnp.dot(own, rows[...], preferred_element_type=jnp.float32)
    total += jnp.dot(from_low, low[...], preferred_element_type=jnp.float32)
    total += jnp.dot(from_high, high[...], preferred_element_type=jnp.float32)
    wide = q_out.shape[1]
    q_out[...] = total[:, :wide].astype(jnp.bfloat16)
    kv_out[...] = total[:, wide:].astype(jnp.bfloat16)
    for copy in copies:
        copy.wait()


def in_hbm(array):
    return pltpu.with_memory_space_constraint(array, pltpu.HBM)


def opening(starts, q, k, v, weight):
    wide = q.shape[1] + k.shape[1] + v.shape[1]
    rows, half = weight.shape[0], weight.shape[1] // 2
    return pl.pallas_call(
        open_kernel,
        out_shape=(bf16(CAP, wide), *(bf16(QUARTER, wide),) * 2, *(bf16(rows, half),) * 2),
        in_specs=[SMEM] + [HBM] * 4,
        out_specs=(VMEM,) * 5,
        scratch_shapes=[pltpu.SemaphoreType.DMA((5,))],
        compiler_params=limit(16),
    )(*(in_hbm(a) for a in (starts, q, k, v, weight)))


def align(starts, own, up, down, parts):
    count = NY * NZ
    low = lax.ppermute(up, ROWS, [(i, (i + 1) % count) for i in range(count)])
    high = lax.ppermute(down, ROWS, [(i, (i - 1) % count) for i in range(count)])
    depth, columns = parts[0].shape
    return pl.pallas_call(
        align_kernel,
        out_shape=(bf16(TOK, HEADS_HERE * HD), bf16(TOK, 2 * HD), bf16(NY * depth, columns)),
        in_specs=[SMEM] + [VMEM] * 7,
        out_specs=(VMEM, VMEM, HBM),
        scratch_shapes=[pltpu.SemaphoreType.DMA((4,))],
        compiler_params=limit(16),
    )(in_hbm(starts), own, low, high, *parts)


def attention_kernel(back, parts, place, lengths, q_ref, *refs):
    blocks, refs = refs[:parts], refs[parts:]
    if back:
        old_stats, old_sums, *refs = refs
    if back == 2:
        out_ref, stats, sums = refs
    else:
        stats, sums = refs
    y, z = place() if callable(place) else place
    ends, total = [], 0
    for i in range(4):
        total += lengths[i]
        ends.append(total)
    mine = y * NZ + z
    query = mine * TOK + lax.broadcasted_iota(jnp.int32, (1, TOK), 1)

    def start_of(token):
        start = token * 0
        for end in ends:
            start = jnp.maximum(start, jnp.where(end <= token, end, 0))
        return start

    starts = start_of(query)
    lowest = start_of(mine * TOK) // TOK
    clear = (start_of(mine * TOK + TOK - 1) + TOK - 1) // TOK

    def step(ref, row, block, masked, opening):
        key, value = ref[pl.ds(row, TOK), :HD], ref[pl.ds(row, TOK), HD:]
        heads = range(HEADS_HERE)
        scores = [
            lax.dot_general(
                key, q_ref[:, h * HD : (h + 1) * HD], (((1,), (1,)), ((), ())), preferred_element_type=jnp.float32
            )
            for h in heads
        ]
        if masked:
            ids = block * TOK + lax.broadcasted_iota(jnp.int32, (TOK, 1), 0)
            allowed = (ids >= starts) & (ids <= query)
            scores = [jnp.where(allowed, s, MASKED) for s in scores]
        tops = [jnp.max(s, axis=0, keepdims=True) * EXP2_SCALE for s in scores]
        if not opening:
            was = [stats[h : h + 1] for h in heads]
            tops = [jnp.maximum(a, b) for a, b in zip(tops, was)]
            fading = [jnp.exp2(a - b) for a, b in zip(was, tops)]
        weights = [jnp.exp2(s * EXP2_SCALE - t) for s, t in zip(scores, tops)]
        mass = [jnp.sum(w, axis=0, keepdims=True) for w in weights]
        added = [
            lax.dot_general(
                value, w.astype(jnp.bfloat16), (((0,), (0,)), ((), ())), preferred_element_type=jnp.float32
            )
            for w in weights
        ]
        if not opening:
            mass = [m + stats[4 + h : 5 + h] * f for h, m, f in zip(heads, mass, fading)]
            added = [a + sums[h] * f for h, a, f in zip(heads, added, fading)]
        for h in heads:
            stats[h : h + 1] = tops[h]
            stats[4 + h : 5 + h] = mass[h]
            sums[h] = added[h]

    if back:
        stats[...] = old_stats[...]
        sums[...] = old_sums[...]
    else:
        step(blocks[0], HERE * TOK, mine, True, True)
    before = 0
    for ref in blocks:

        def body(i, _, ref=ref, before=before):
            block = (y - back) * NZ + lax.rem(z + before + i - HERE + NZ, NZ)
            needed = (block >= lowest) & (block < mine)
            row = pl.multiple_of(i * TOK, TOK)

            @pl.when(needed & (block < clear))
            def _():
                step(ref, row, block, True, False)

            @pl.when(needed & (block >= clear))
            def _():
                step(ref, row, block, False, False)

            return 0

        lax.fori_loop(0, ref.shape[0] // TOK, body, 0)
        before += ref.shape[0] // TOK
    if back == 2:
        for h in range(HEADS_HERE):
            out_ref[:, h * HD : (h + 1) * HD] = (sums[h] / stats[4 + h : 5 + h]).T.astype(jnp.bfloat16)


def attention(back, lengths, q, blocks, state, place=lambda: here()[:2]):
    shapes = [f32(2 * HEADS_HERE, TOK), f32(HEADS_HERE, HD, TOK)]
    kwargs = {}
    if back == 2:
        kwargs["scratch_shapes"] = [pltpu.VMEM(s.shape, s.dtype) for s in shapes]
        shapes = [bf16(TOK, HEADS_HERE * HD)]
    work = 8 * HEADS_HERE * TOK * TOK
    return pl.pallas_call(
        functools.partial(attention_kernel, back, len(blocks), place),
        out_shape=tuple(shapes),
        in_specs=[SMEM] + [VMEM] * (1 + len(blocks) + len(state)),
        out_specs=(VMEM,) * len(shapes),
        compiler_params=limit(32),
        cost_estimate=pl.CostEstimate(flops=4 * work * HD, bytes_accessed=4 << 20, transcendentals=work),
        **kwargs,
    )(lengths, q, *blocks, *state)


def prepare_kernel(gain, mine, other, rows, inv):
    y, _, x, c = here()
    squares = jnp.zeros((TOK, HD), jnp.float32)
    for side, pieces in enumerate((mine, other)):
        for i in range(NX):
            tp = lax.rem(x + (0, 3, 1, 2)[i], NX) * NC + (c if side == 0 else 1 - c)
            for j in range(HEADS_HERE):
                head = tp * HEADS_HERE + j
                part = pieces[i * TOK : (i + 1) * TOK, j * HD : (j + 1) * HD].astype(jnp.float32)
                squares += part * part
                scaled = (part * gain[:, pl.ds(pl.multiple_of(head * HD, HD), HD)]).astype(jnp.bfloat16)
                away = lax.rem(head // NZ - y + NY, NY)
                slot = jnp.where(away == 0, 0, jnp.where(away == 3, 1, away + 1))
                place = lax.rem(head, NZ) * NY + slot
                rows[:, pl.ds(pl.multiple_of(place * HD, HD), HD)] = scaled
    mean = jnp.sum(squares, axis=1, keepdims=True) / FEATURES
    inv[...] = jnp.broadcast_to(lax.rsqrt(mean + NORM_EPS), (TOK, HD))


def prepare(gain, mine, other):
    return pl.pallas_call(
        prepare_kernel,
        out_shape=(bf16(TOK, FEATURES), f32(TOK, HD)),
        in_specs=[VMEM] * 3,
        out_specs=(VMEM,) * 2,
        compiler_params=limit(16),
    )(gain, mine, other)


def silu(value):
    return (value / (1.0 + jnp.exp(-value))).astype(jnp.bfloat16)


def first_gate_kernel(rows, inv, weight, out, held, total, sems):
    depth = FEATURES // PARTS
    sent = out.shape[1]
    parts = [pl.ds(i * depth, depth) for i in range(PARTS)]
    spots = [(p, c) for c in (pl.ds(0, sent), pl.ds(sent, held.shape[1] - sent)) for p in parts]
    copies = [pltpu.make_async_copy(weight.at[s], held.at[s], sems.at[i]) for i, s in enumerate(spots)]
    for copy in copies:
        copy.start()
    for i in range(PARTS):
        copies[i].wait()
        term = jnp.dot(
            rows[:, i * depth : (i + 1) * depth],
            held[i * depth : (i + 1) * depth, :sent],
            preferred_element_type=jnp.float32,
        )
        if i == 0:
            total[...] = term
        elif i < PARTS - 1:
            total[...] += term
        else:
            out[...] = silu((total[...] + term) * inv[:, :1])
    for copy in copies[PARTS:]:
        copy.wait()


def first_gate(rows, inv, weight):
    return pl.pallas_call(
        first_gate_kernel,
        out_shape=(bf16(TOK, SENT_FIRST), bf16(*weight.shape)),
        in_specs=[VMEM] * 2 + [HBM],
        out_specs=(VMEM,) * 2,
        scratch_shapes=[pltpu.VMEM((TOK, SENT_FIRST), jnp.float32), pltpu.SemaphoreType.DMA((2 * PARTS,))],
        compiler_params=limit(20),
    )(rows, inv, in_hbm(weight))


def gate_kernel(first, rows, inv, weight, out):
    for at in range(0, out.shape[1], 2 * HD):
        end = min(at + 2 * HD, out.shape[1])
        value = jnp.dot(rows[...], weight[:, first + at : first + end], preferred_element_type=jnp.float32)
        out[:, at:end] = silu(value * inv[:, :1])


def gate(rows, inv, weight, first, columns):
    return pl.pallas_call(
        functools.partial(gate_kernel, first),
        out_shape=bf16(TOK, columns),
        in_specs=[VMEM] * 3,
        out_specs=VMEM,
        compiler_params=limit(20),
        cost_estimate=pl.CostEstimate(
            flops=2 * TOK * FEATURES * columns, bytes_accessed=2 * FEATURES * columns, transcendentals=TOK * columns
        ),
    )(rows, inv, weight)


def join_kernel(*refs):
    *parts, out = refs
    half, odd = out.shape[1] // 2, lax.rem(here()[0], 2)
    at = 0
    for ref in parts:
        side = odd if at < half else 1 - odd
        place = side * half + at % half
        out[:, pl.ds(pl.multiple_of(place, HD), ref.shape[1])] = ref[...]
        at += ref.shape[1]


def join(*parts):
    return pl.pallas_call(
        join_kernel,
        out_shape=bf16(TOK, sum(part.shape[1] for part in parts)),
        in_specs=[VMEM] * len(parts),
        out_specs=VMEM,
        compiler_params=limit(8),
    )(*parts)


def on_device(queries, keys, values, doc_lengths, shard_starts, norm_gain, ffn_weight):
    with jax.named_scope("rows_to_owners"):
        own, up, down, theirs, mine = opening(shard_starts, queries, keys, values, ffn_weight)
        far_part = shift(mine, TALL, 2)
        parts = [mine, shift(theirs, TALL, 1), shift(theirs, TALL, -1), far_part]
        q, kv, pair = align(shard_starts, own, up, down, parts)

    with jax.named_scope("weight_rows"):
        weight = lax.all_gather(pair, "z", axis=0, tiled=True)

    with jax.named_scope("keys_and_values"):
        far, near = z_blocks(kv)
        far1, near1 = (hop(a, (0, 1), (1, 2), (2, 3)) for a in (far, near))
        outer, inner = far[: HERE * TOK], far[HERE * TOK :]
        inner2 = hop(hop(inner, (1, 0), (0, 3)), (3, 2), (0, 3))
        outer2 = hop(hop(outer, (1, 0), (0, 3), below=HERE), (3, 2), (0, 3), below=HERE)
        state = attention(0, doc_lengths, q, [far, near], ())
        near1, far1, *state = lax.optimization_barrier((near1, far1, *state))
        near2 = hop(near1, (1, 2), (2, 3), below=FAR)

    with jax.named_scope("attention"):
        state = attention(1, doc_lengths, q, [far1, near1], state)
        (attended,) = attention(2, doc_lengths, q, [outer2, inner2, near2], state)

    gain = norm_gain.reshape(1, FEATURES)
    half = weight.shape[1]
    with jax.named_scope("features"):
        theirs = [shift_both(attended, 1, d) for d in (0, 1, -1, 2)]
        own = [attended] + [shift(attended, "x", d) for d in (1, -1, 2)]
        theirs, own = jnp.concatenate(theirs, axis=0), jnp.concatenate(own, axis=0)
        their_rows, their_inv = prepare(gain, theirs, shift(theirs, "c", 1))
        other = shift(own, "c", 1)

    with jax.named_scope("gate"):
        away, held = first_gate(their_rows, their_inv, weight)
        back = [shift(away, "yb", 1)]
        their_inv, away = lax.optimization_barrier((their_inv, away))
        rest = gate(their_rows, their_inv, held, SENT_FIRST, half - SENT_FIRST)
        back.append(shift(rest, "yb", 1))
        gain, rest = lax.optimization_barrier((gain, rest))
        home = gate(*prepare(gain, own, other), held, 0, half)
        return join(home, *back)


def solution(mesh):
    fine = Mesh(mesh.devices.reshape(NY // 2, 2, NZ, NX, NC), ("yp", "yb", "z", "x", "c"))
    return jax.shard_map(
        on_device,
        mesh=fine,
        in_specs=(P(ROWS, COLUMNS), P(ROWS, COLUMNS), P(ROWS, COLUMNS), P(), P(), P(), P(ROWS, COLUMNS)),
        out_specs=P(ROWS, COLUMNS),
        check_vma=False,
    )
```
